1024 devices in a mesh: dp: 64 (over z, core), replica: 16 (over y, x).
Axes of the slice: x: 4, y: 4, z: 32, core: 2. Of those that a mesh axis runs over, the one named last changes fastest.
Arguments:
- events: bfloat16 [262144, 512], P(('dp', 'replica')), may hold values from -24 to 24
- out_grad: bfloat16 [262144, 512], P(('dp', 'replica')), may hold values from -6 to 6
- in_proj: float32 [512, 1536], replicated, may hold values from -0.25 to 0.25
- out_proj: float32 [512, 512], replicated, may hold values from -0.25 to 0.25
- lengths: int32 [64, 16, 65], P(None, 'replica'), may hold values from 1 to 128, as said below
- offsets: int32 [64, 16, 65], P(None, 'replica'), may hold values from 0 to 254, as said below
- targets: int32 [64, 16, 65], P(None, 'replica'), may hold values from 0 to 63, as said below
Outputs:
- input_grad: float32 [262144, 512], P(('dp', 'replica'))
- packed_grad: float32 [131072, 512], P(('dp', 'replica'))
- grad_in_proj: float32 [512, 1536], P('dp')
- grad_out_proj: float32 [512, 512], P('dp')
The draws below stay inside these ranges and needn't reach their ends.
Inputs may be any that keep to these rules, and one draw needn't show every extreme that they name: `lengths`: user 0 of every device is its long user, of 3 to 128 events; users 1 to 64 are its short users, of 1 to 2 events. In one replica index every short user has exactly 2 events. `offsets`: the long user begins at row 0; short user u begins at row 1 * 128 + 2 * k, where k runs over a permutation of 0 to 63 on each device. The long user's target is its own dp index; the 64 short users of a device have 64 different targets.
All inputs are finite; a program needn't handle non-finite values.
Results may differ from the reference program's by a relative error of at most 0.024.
Values may be sent and summed in bfloat16 or wider, within the bound.
A program may use at most 32 MiB of HBM per device.

```python
import jax
import jax.numpy as jnp
from jax import lax

D = 512
HEADS = 4
QK_DIM = 64
VDIM = 128
TILE = 128
CAP = 2
LONG = 1
USERS = 65
ROWS = 256
F1 = 1536
N_DP = 64
N_REPLICA = 16


def user_layout(key):
    key_list = jax.random.split(key, 5)
    long_rows = LONG * TILE
    long_length = jax.random.randint(key_list[0], (N_DP, N_REPLICA, 1), CAP + 1, long_rows + 1)
    long_length = long_length.at[0, 0, 0].set(long_rows)
    short_length = jax.random.randint(key_list[1], (N_DP, N_REPLICA, N_DP), 1, CAP + 1)
    full_group = jax.random.randint(key_list[2], (), 0, N_REPLICA)
    group_ids = jnp.arange(N_REPLICA)[None, :, None]
    short_length = jnp.where(group_ids == full_group, CAP, short_length)
    lengths = jnp.concatenate([long_length, short_length], axis=2).astype(jnp.int32)
    lane_ids = jnp.arange(N_DP)
    slot_scores = jax.random.randint(key_list[3], (N_DP, N_REPLICA, N_DP), 0, 1 << 20) * N_DP + lane_ids
    slot_ids = jnp.argsort(slot_scores, axis=2, stable=True)
    offsets = jnp.concatenate([jnp.zeros((N_DP, N_REPLICA, 1), jnp.int32), (long_rows + CAP * slot_ids).astype(jnp.int32)], axis=2)
    target_scores = jax.random.randint(key_list[4], (N_DP, N_REPLICA, N_DP), 0, 1 << 20) * N_DP + lane_ids
    short_target = jnp.argsort(target_scores, axis=2, stable=True)
    home_index = jnp.broadcast_to(lane_ids[:, None, None], (N_DP, N_REPLICA, 1))
    targets = jnp.concatenate([home_index, short_target], axis=2).astype(jnp.int32)
    return (lengths, offsets.astype(jnp.int32), targets)


def draw_lengths(key, part):
    shared = user_layout(key)
    return shared[0]


def draw_offsets(key, part):
    shared = user_layout(key)
    return shared[1]


def draw_targets(key, part):
    shared = user_layout(key)
    return shared[2]


def strengthened(result, key, source, target, blocks, factor):
    def block_of(position):
        return (jnp.arange(result.shape[position]) // (result.shape[position] // blocks)).reshape((-1,) + (1,) * (result.ndim - 1 - position))

    first = jax.random.permutation(key, blocks)[block_of(target)]
    second = (block_of(target) + blocks // 2) % blocks
    return jnp.where((block_of(source) == first) | (block_of(source) == second), factor * result, result)


def shard_levels(stream_key, extent, cuts, smallest, largest):
    def one(position, parts):
        heights = jax.random.uniform(jax.random.fold_in(jax.random.fold_in(stream_key, 6), position), (parts,), jnp.float32, smallest / len(cuts), largest / len(cuts))
        return jnp.repeat(jnp.exp(heights), extent[position] // parts).reshape((-1,) + (1,) * (len(extent) - position - 1))

    loudness = one(*cuts[0])
    for cut in cuts[1:]:
        loudness = loudness * one(*cut)
    return loudness


def noise(key, extent, scale, reach, cuts=(), held_as=jnp.bfloat16):
    entries = scale * jax.random.normal(key, extent, jnp.float32)
    if cuts:
        entries = entries * shard_levels(key, extent, cuts, -0.22, 0.18)
    return jnp.clip(entries, -reach, reach).astype(held_as)


def heavy_noise(key, dims, scale, limit, cuts, heavy, held_as=jnp.bfloat16):
    result = scale * jax.random.normal(key, dims, jnp.float32)
    if cuts:
        result = result * shard_levels(key, dims, cuts, -0.22, 0.18)
    return jnp.clip(strengthened(result, jax.random.fold_in(key, 3), *heavy), -limit, limit).astype(held_as)


def setup_inputs(seed: int = 0) -> dict:
    arg_keys = jax.random.split(jax.random.key(seed), 8)
    return {
        "events": heavy_noise(arg_keys[0], (N_DP * N_REPLICA * ROWS, D), 1.0, 24.0, ((0, 1024),), (0, 1, 512, 6.0)),
        "out_grad": noise(arg_keys[1], (N_DP * N_REPLICA * ROWS, D), 1.0, 6.0, ((0, 1024),)),
        "in_proj": noise(arg_keys[2], (D, F1), D ** -0.5, 0.25, (), jnp.float32),
        "out_proj": noise(arg_keys[3], (D, D), D ** -0.5, 0.25, (), jnp.float32),
        "lengths": draw_lengths(jax.random.fold_in(arg_keys[7], 71), 0),
        "offsets": draw_offsets(jax.random.fold_in(arg_keys[7], 71), 0),
        "targets": draw_targets(jax.random.fold_in(arg_keys[7], 71), 0),
    }


def row_norm(values):
    centered = values - lax.optimization_barrier(jnp.mean(values, axis=-1, keepdims=True))
    return centered / jnp.sqrt(lax.optimization_barrier(jnp.mean(centered * centered, axis=-1, keepdims=True)) + 1e-05)

def norm_cast(values):
    return row_norm(values).astype(jnp.bfloat16)

def bf_round(values):
    return lax.optimization_barrier(values.astype(jnp.bfloat16)).astype(jnp.float32)

def long_layout(length, width):
    row_pos = jnp.arange(width).astype(jnp.int32)
    row_len = jnp.zeros((width,), jnp.int32) + length
    return (row_len, row_pos, jnp.zeros((width,), jnp.int32))

def pool_layout(slot_lengths):
    width = slot_lengths.shape[0] * CAP
    rows_idx = jnp.arange(width).astype(jnp.int32)
    row_seg = (rows_idx // CAP).astype(jnp.int32)
    row_pos = (rows_idx % CAP).astype(jnp.int32)
    lanes = jnp.arange(slot_lengths.shape[0]).astype(jnp.int32)
    row_len = lax.optimization_barrier(jnp.sum(jnp.where(row_seg[:, None] == lanes[None, :], slot_lengths[None, :], 0), axis=1)).astype(jnp.int32)
    return (row_len, row_pos, row_seg)

def attend(projected, row_len, row_pos, row_seg):
    row_count = projected.shape[0]
    qk_width = HEADS * QK_DIM
    activated = jax.nn.silu(projected)
    gate_u = activated[:, :D]
    value_rows = bf_round(activated[:, D:2 * D]).reshape(row_count, HEADS, VDIM)
    query_rows = bf_round(activated[:, 2 * D:2 * D + qk_width]).reshape(row_count, HEADS, QK_DIM)
    key_rows = bf_round(activated[:, 2 * D + qk_width:]).reshape(row_count, HEADS, QK_DIM)
    scores = jnp.einsum('ihd,jhd->hij', query_rows, key_rows) * QK_DIM ** (-0.5)
    keep_pair = (row_seg[None, :] == row_seg[:, None]) & (row_pos[None, :] <= row_pos[:, None]) & (row_pos < row_len)[:, None]
    divisor = jnp.maximum(row_len, 1).astype(jnp.float32)[None, :, None]
    weights = jnp.where(keep_pair[None], jax.nn.silu(scores) / divisor, 0.0)
    weights = bf_round(weights)
    mixed_rows = jnp.einsum('hij,jhd->ihd', weights, value_rows).reshape(row_count, D)
    return (gate_u * row_norm(mixed_rows)).astype(jnp.bfloat16)

def block_pass(rows_in, grad_block, layout, w_in, w_out):
    row_len, row_pos, row_seg = layout
    live_rows = row_pos < row_len
    grad_live = jnp.where(live_rows[:, None], grad_block, jnp.zeros_like(grad_block))
    normed, norm_back = jax.vjp(norm_cast, rows_in.astype(jnp.float32))
    projected = jnp.dot(normed, w_in, preferred_element_type=jnp.float32)
    hidden, core_back = jax.vjp(lambda value_in: attend(value_in, row_len, row_pos, row_seg), projected)
    dhidden = jnp.dot(grad_live, w_out.T, preferred_element_type=jnp.float32).astype(jnp.bfloat16)
    grad_proj = core_back(dhidden)[0].astype(jnp.bfloat16)
    dnormed = jnp.dot(grad_proj, w_in.T, preferred_element_type=jnp.float32).astype(jnp.bfloat16)
    grad_rows = norm_back(dnormed)[0] + grad_live.astype(jnp.float32)
    grad_rows = jnp.where(live_rows[:, None], grad_rows, 0.0)
    return (grad_rows, normed, grad_proj, hidden, grad_live)

def reference(events, out_grad, in_proj, out_proj, lengths, offsets, targets):
    w_in = in_proj.astype(jnp.bfloat16)
    w_out = out_proj.astype(jnp.bfloat16)
    long_rows = LONG * TILE
    block_rows = long_rows + N_DP * CAP
    device_count = N_DP * N_REPLICA
    event_blocks = events.reshape(device_count, block_rows, D)
    grad_blocks = out_grad.reshape(device_count, block_rows, D)
    length_rows = lengths.reshape(device_count, USERS)
    offset_rows = offsets.reshape(device_count, USERS)
    target_rows = targets.reshape(device_count, USERS)
    lane_ids = jnp.arange(N_DP).astype(jnp.int32)

    def one_block(running, step_item):
        rows_in, grad_block, block_lengths, block_offsets, block_targets = step_item
        long_pass = block_pass(rows_in[:long_rows], grad_block[:long_rows], long_layout(block_lengths[0], long_rows), w_in, w_out)
        slot_ids = ((block_offsets[1:] - long_rows) // CAP).astype(jnp.int32)
        owner_mask = slot_ids[None, :] == lane_ids[:, None]
        slot_lengths = lax.optimization_barrier(jnp.sum(jnp.where(owner_mask, block_lengths[None, 1:], 0), axis=1)).astype(jnp.int32)
        pool_pass = block_pass(rows_in[long_rows:], grad_block[long_rows:], pool_layout(slot_lengths), w_in, w_out)
        in_term = jnp.dot(long_pass[1].T, long_pass[2], preferred_element_type=jnp.float32)
        in_term = in_term + jnp.dot(pool_pass[1].T, pool_pass[2], preferred_element_type=jnp.float32)
        out_term = jnp.dot(long_pass[3].T, long_pass[4], preferred_element_type=jnp.float32)
        out_term = out_term + jnp.dot(pool_pass[3].T, pool_pass[4], preferred_element_type=jnp.float32)
        target_mask = block_targets[None, 1:] == lane_ids[:, None]
        slot_of_target = lax.optimization_barrier(jnp.sum(jnp.where(target_mask, slot_ids[None, :], 0), axis=1)).astype(jnp.int32)
        delivered = pool_pass[0].reshape(N_DP, CAP, D)[slot_of_target]
        home_grad = jnp.concatenate([long_pass[0], jnp.zeros((N_DP * CAP, D), jnp.float32)], axis=0)
        return ((running[0] + in_term, running[1] + out_term), (home_grad, delivered))
    start_sums = (jnp.zeros((D, F1), jnp.float32), jnp.zeros((D, D), jnp.float32))
    sums, outputs = lax.scan(one_block, start_sums, (event_blocks, grad_blocks, length_rows, offset_rows, target_rows))
    home_grad, delivered = outputs
    moved_grad = delivered.reshape(N_DP, N_REPLICA, N_DP, CAP, D).transpose(2, 1, 0, 3, 4).reshape(-1, D)
    return (home_grad.reshape(-1, D), moved_grad, sums[0], sums[1])
```

```python
import functools

import jax
import jax.numpy as jnp
from jax import lax
from jax.experimental import pallas as pl
from jax.experimental.pallas import tpu as pltpu
from jax.sharding import PartitionSpec as P

D = 512
HEADS = 4
TILE = 128
CAP = 2
F1 = 1536
LANES = 128
SUB = 8
MESH = pl.DeviceIdType.MESH
F32 = jnp.float32
BF16 = jnp.bfloat16

NT = (((1,), (1,)), ((), ()))
TN = (((0,), (0,)), ((), ()))


def dot(a, b, dims=(((1,), (0,)), ((), ()))):
    return lax.dot_general(a, b, dims, preferred_element_type=F32)


def sigmoid(v):
    return 0.5 * jnp.tanh(0.5 * v) + 0.5


def mean_rows(v):
    return jnp.mean(v, axis=-1, keepdims=True)


def row_norm(v):
    centered = v - mean_rows(v)
    scale = lax.rsqrt(mean_rows(centered * centered) + 1e-05)
    return centered * scale, scale


def norm_back(grad, unit, scale):
    return scale * (grad - mean_rows(grad) - unit * mean_rows(grad * unit))


def compute_kernel(
    ev, og, wi, wo, ln, of, tg, home, send, parts,
    wib, wob, slope, gate, val, qry, key, wts, wslope, mixed, dproj, spread,
):
    me = lax.axis_index("dp")
    ln_row, of_row, tg_row = ln[me], of[me], tg[me]
    users = ln_row.shape[1]
    rows = lax.broadcasted_iota(jnp.int32, (TILE, 1), 0)
    lanes = lax.broadcasted_iota(jnp.int32, (1, users), 1)
    pair = lax.div(rows, CAP)
    at_slot = (of_row - TILE) == pair * CAP
    pool_len = jnp.sum(jnp.where(at_slot, ln_row, 0), axis=1, keepdims=True)
    long_len = jnp.broadcast_to(ln_row[:, 0:1], (TILE, 1))
    live_long = rows < long_len
    live_pool = lax.rem(rows, CAP) < pool_len

    for n in range(0, F1, 256):
        wib[:, n : n + 256] = wi[:, n : n + 256].astype(BF16)
    wob[...] = wo[...].astype(BF16)

    live = jnp.concatenate([live_long, live_pool], axis=0)
    unit, scale = row_norm(ev[...].astype(F32))
    normed = unit.astype(BF16)
    grad_live = jnp.where(live, og[...].astype(F32), 0.0)
    grad_b = grad_live.astype(BF16)

    for n in range(0, F1, 256):
        proj = dot(normed, wib[:, n : n + 256])
        sig = sigmoid(proj)
        act = proj * sig
        slope[:, n : n + 256] = sig + act * (1.0 - sig)
        if n < D:
            gate[:, n : n + 256] = act
        elif n < 2 * D:
            val[:, n - D : n - D + 256] = act.astype(BF16)
        elif n < 2 * D + 256:
            qry[...] = act.astype(BF16)
        else:
            key[...] = act.astype(BF16)

    cols = lax.broadcasted_iota(jnp.int32, (TILE, TILE), 1)
    row2 = lax.broadcasted_iota(jnp.int32, (TILE, TILE), 0)
    low = lax.broadcasted_iota(jnp.int32, (TILE, LANES), 1) < 64
    zero_b = jnp.zeros((TILE, LANES), BF16)
    for b in range(2):
        top = b * TILE
        keep = cols <= row2
        if b == 0:
            keep = keep & live_long
            size = long_len
        else:
            keep = keep & (lax.div(cols, CAP) == lax.div(row2, CAP)) & live_pool
            size = pool_len
        inv = 1.0 / jnp.maximum(size, 1).astype(F32)
        for h in range(HEADS):
            lane = (h // 2) * LANES
            mine = low if h % 2 == 0 else ~low
            qh = jnp.where(mine, qry[top : top + TILE, lane : lane + LANES], zero_b)
            score = dot(qh, key[top : top + TILE, lane : lane + LANES], NT) * 0.125
            sig = sigmoid(score)
            act = score * sig
            w = jnp.where(keep, act * inv, 0.0).astype(BF16)
            wts[b * HEADS + h] = w
            wslope[b * HEADS + h] = jnp.where(
                keep, (sig + act * (1.0 - sig)) * (inv * 0.125), 0.0
            )
            mixed[top : top + TILE, h * LANES : (h + 1) * LANES] = dot(
                w, val[top : top + TILE, h * LANES : (h + 1) * LANES]
            )

    unit_m, scale_m = row_norm(mixed[...])
    gate_u = gate[...]
    hidden = (gate_u * unit_m).astype(BF16)
    dhid = dot(grad_b, wob[...], NT).astype(BF16).astype(F32)
    dproj[:, :D] = (dhid * unit_m * slope[:, :D]).astype(BF16)
    dmix = norm_back(dhid * gate_u, unit_m, scale_m).astype(BF16)

    def emit(result, first):
        groups = result.shape[0] // (2 * SUB)
        for i in range(result.shape[1] // LANES):
            piece = result[:, i * LANES : (i + 1) * LANES].reshape(
                groups, 2, SUB, LANES
            )
            for c in range(2):
                parts[c, first + i] = (
                    piece[:, c].reshape(groups * SUB, LANES).astype(BF16)
                )

    hidden_t = hidden.T
    for n in range(0, D, 256):
        emit(dot(hidden_t, grad_b[:, n : n + 256]), (F1 + n) // LANES)

    for b in range(2):
        top = b * TILE
        for p in range(HEADS // 2):
            lane = p * LANES
            kk = key[top : top + TILE, lane : lane + LANES]
            qq = qry[top : top + TILE, lane : lane + LANES]
            dq, dk = [], []
            for h in (2 * p, 2 * p + 1):
                dm = dmix[top : top + TILE, h * LANES : (h + 1) * LANES]
                vh = val[top : top + TILE, h * LANES : (h + 1) * LANES]
                w = wts[b * HEADS + h]
                dw = dot(dm, vh, NT).astype(BF16).astype(F32)
                dv = dot(w, dm, TN).astype(BF16).astype(F32)
                at = D + h * LANES
                dproj[top : top + TILE, at : at + LANES] = (
                    dv * slope[top : top + TILE, at : at + LANES]
                ).astype(BF16)
                ds = (dw * wslope[b * HEADS + h]).astype(BF16)
                dq.append(dot(ds, kk))
                dk.append(dot(ds, qq, TN))
            for at, pieces in ((2 * D + lane, dq), (2 * D + 256 + lane, dk)):
                both = jnp.where(low, pieces[0], pieces[1]).astype(BF16).astype(F32)
                dproj[top : top + TILE, at : at + LANES] = (
                    both * slope[top : top + TILE, at : at + LANES]
                ).astype(BF16)

    normed_t = normed.T
    for n in range(0, F1, 256):
        emit(dot(normed_t, dproj[:, n : n + 256]), n // LANES)

    dnormed = dot(dproj[...], wib[...], NT).astype(BF16).astype(F32)
    grad = norm_back(dnormed, unit, scale) + grad_live
    grad = jnp.where(live, grad, 0.0)
    home[:TILE] = grad[:TILE]
    home[TILE:] = jnp.zeros((TILE, D), F32)

    to_target = ((tg_row == pair) & (lanes >= 1)).astype(F32).astype(BF16)
    from_slot = at_slot.astype(F32).astype(BF16)
    moves = dot(to_target, from_slot, NT)
    moves = jnp.where(lax.rem(cols, CAP) == lax.rem(row2, CAP), moves, 0.0)
    packed = dot(moves.astype(BF16), grad[TILE:].astype(BF16))
    for i in range(D // LANES):
        spread[pl.ds(i, TILE, stride=D // LANES), :] = packed[
            :, i * LANES : (i + 1) * LANES
        ]
    send[...] = spread[...].reshape(send.shape).astype(BF16)


def comm_kernel(
    n_dp, n_rep, send, parts, packed, grads,
    got, core_in, chip, rep_in, acc, z_out, z_in, fin, fin_in, spread,
    pk_s, pk_r, c_s, c_r, r_s, r_r, z_s, z_r, f_s, f_r,
):
    me = lax.axis_index("dp")
    rep = lax.axis_index("replica")
    nz = n_dp // 2
    core = lax.rem(me, 2)
    z = lax.div(me, 2)
    other = me + 1 - 2 * core

    barrier = pltpu.get_barrier_semaphore()

    def dp_peer(k):
        return lax.rem(me + k, n_dp)

    def rep_peer(k):
        return lax.rem(rep + k, n_rep)

    def z_peer(k):
        return lax.rem(z + k, nz)

    @pl.loop(1, n_dp)
    def _(k):
        pl.semaphore_signal(
            barrier, inc=1, device_id=(dp_peer(k), rep), device_id_type=MESH
        )

    @pl.loop(1, n_rep)
    def _(k):
        pl.semaphore_signal(
            barrier, inc=1, device_id=(me, rep_peer(k)), device_id_type=MESH
        )

    pl.semaphore_wait(barrier, n_dp - 1 + n_rep - 1)

    def core_copy(r):
        return pltpu.make_async_remote_copy(
            src_ref=parts.at[1 - core, r],
            dst_ref=core_in.at[r],
            send_sem=c_s.at[r],
            recv_sem=c_r.at[r],
            device_id=(other, rep),
            device_id_type=MESH,
        )

    def rep_copy(r, slot):
        return pltpu.make_async_remote_copy(
            src_ref=chip.at[r],
            dst_ref=rep_in.at[slot],
            send_sem=r_s.at[r],
            recv_sem=r_r.at[slot],
            device_id=(me, r),
            device_id_type=MESH,
        )

    def packed_copy(t):
        return pltpu.make_async_remote_copy(
            src_ref=send.at[t],
            dst_ref=got.at[me],
            send_sem=pk_s,
            recv_sem=pk_r,
            device_id=(t, rep),
            device_id_type=MESH,
        )

    def z_copy(t):
        return pltpu.make_async_remote_copy(
            src_ref=z_out.at[t],
            dst_ref=z_in.at[z],
            send_sem=z_s,
            recv_sem=z_r,
            device_id=(t * 2 + core, rep),
            device_id_type=MESH,
        )

    def fin_copy(r):
        return pltpu.make_async_remote_copy(
            src_ref=fin,
            dst_ref=fin_in.at[rep],
            send_sem=f_s.at[r],
            recv_sem=f_r,
            device_id=(me, r),
            device_id_type=MESH,
        )

    def wait_all(ref, count, sem):
        part = ref.at[pl.ds(0, count)]
        pltpu.make_async_copy(part, part, sem).wait()

    @pl.loop(1, n_rep + 1)
    def _(k):
        core_copy(rep_peer(k)).start()

    @pl.loop(1, n_dp)
    def _(k):
        packed_copy(dp_peer(k)).start()

    got[me] = send[me]

    @pl.loop(1, n_rep)
    def _(k):
        r = rep_peer(k)
        core_copy(r).wait_recv()
        chip[r] = (parts[core, r].astype(F32) + core_in[r].astype(F32)).astype(BF16)
        rep_copy(r, rep).start()

    core_copy(rep).wait_recv()
    acc[...] = parts[core, rep].astype(F32) + core_in[rep].astype(F32)

    @pl.loop(1, n_rep)
    def _(k):
        r = rep_peer(n_rep - k)
        rep_copy(r, r).wait_recv()
        acc[...] += rep_in[r].astype(F32)

    z_out[...] = acc[...].reshape(z_out.shape).astype(BF16)

    @pl.loop(1, nz)
    def _(k):
        z_copy(z_peer(k)).start()

    z_in[z] = z_out[z]
    wait_all(z_in, nz - 1, z_r)
    fin[...] = jnp.sum(z_in[...].astype(F32), axis=0)

    @pl.loop(1, n_rep)
    def _(k):
        fin_copy(rep_peer(k)).start()

    fin_in[rep] = fin[...]

    wait_all(got, n_dp - 1, pk_r)
    spread[...] = got[...].astype(F32).reshape(spread.shape)
    for i in range(D // LANES):
        packed[:, i * LANES : (i + 1) * LANES] = spread[
            pl.ds(i, packed.shape[0], stride=D // LANES), :
        ]

    wait_all(fin_in, n_rep - 1, f_r)
    for r in range(n_rep):
        grads[:, r * LANES : (r + 1) * LANES] = fin_in[r]

    @pl.loop(1, n_rep + 1)
    def _(k):
        core_copy(rep_peer(k)).wait_send()

    @pl.loop(1, n_rep)
    def _(k):
        rep_copy(rep_peer(k), rep).wait_send()
        fin_copy(rep_peer(k)).wait_send()

    wait_all(send, n_dp - 1, pk_s)
    wait_all(z_out, nz - 1, z_s)


def vmem():
    return pl.BlockSpec(memory_space=pltpu.VMEM)


def compute(events, out_grad, in_proj, out_proj, lengths, offsets, targets, n_dp, n_rep):
    rows = events.shape[0]
    half = D // 2
    return pl.pallas_call(
        compute_kernel,
        out_shape=(
            jax.ShapeDtypeStruct((rows, D), F32),
            jax.ShapeDtypeStruct((n_dp, SUB, LANES), BF16),
            jax.ShapeDtypeStruct((2, (F1 + D) // LANES, half, LANES), BF16),
        ),
        in_specs=[vmem()] * 7,
        out_specs=(vmem(), vmem(), vmem()),
        scratch_shapes=[
            pltpu.VMEM((D, F1), BF16),
            pltpu.VMEM((D, D), BF16),
            pltpu.VMEM((rows, F1), F32),
            pltpu.VMEM((rows, D), F32),
            pltpu.VMEM((rows, D), BF16),
            pltpu.VMEM((rows, 256), BF16),
            pltpu.VMEM((rows, 256), BF16),
            pltpu.VMEM((2 * HEADS, TILE, TILE), BF16),
            pltpu.VMEM((2 * HEADS, TILE, TILE), F32),
            pltpu.VMEM((rows, D), F32),
            pltpu.VMEM((rows, F1), BF16),
            pltpu.VMEM((TILE * D // LANES, LANES), F32),
        ],
        compiler_params=pltpu.CompilerParams(vmem_limit_bytes=48 * 2**20),
        name="rows",
    )(events, out_grad, in_proj, out_proj, lengths, offsets, targets)


def exchange(send, parts, n_dp, n_rep):
    nz = n_dp // 2
    deep = parts.shape[2]
    dma = pltpu.SemaphoreType.DMA
    return pl.pallas_call(
        functools.partial(comm_kernel, n_dp, n_rep),
        out_shape=(
            jax.ShapeDtypeStruct((n_dp * CAP, D), F32),
            jax.ShapeDtypeStruct((SUB, n_rep * LANES), F32),
        ),
        in_specs=[vmem()] * 2,
        out_specs=(vmem(), vmem()),
        scratch_shapes=[
            pltpu.VMEM((n_dp, SUB, LANES), BF16),
            pltpu.VMEM((n_rep, deep, LANES), BF16),
            pltpu.VMEM((n_rep, deep, LANES), BF16),
            pltpu.VMEM((n_rep, deep, LANES), BF16),
            pltpu.VMEM((deep, LANES), F32),
            pltpu.VMEM((nz, SUB, LANES), BF16),
            pltpu.VMEM((nz, SUB, LANES), BF16),
            pltpu.VMEM((SUB, LANES), F32),
            pltpu.VMEM((n_rep, SUB, LANES), F32),
            pltpu.VMEM((n_dp * SUB, LANES), F32),
            dma, dma,
            dma((n_rep,)), dma((n_rep,)),
            dma((n_rep,)), dma((n_rep,)),
            dma, dma,
            dma((n_rep,)), dma,
        ],
        compiler_params=pltpu.CompilerParams(
            collective_id=0, has_side_effects=True, vmem_limit_bytes=32 * 2**20
        ),
        name="exchange",
    )(send, parts)


def on_device(n_dp, n_rep, *args):
    home, send, parts = compute(*args, n_dp, n_rep)
    packed, grads = exchange(send, parts, n_dp, n_rep)
    return home, packed, grads[:, :F1], grads[:, F1:]


def solution(mesh):
    in_specs = (
        P(("dp", "replica"), None),
        P(("dp", "replica"), None),
        P(),
        P(),
        P(None, "replica", None),
        P(None, "replica", None),
        P(None, "replica", None),
    )
    out_specs = (
        P(("dp", "replica"), None),
        P(("dp", "replica"), None),
        P("dp", None),
        P("dp", None),
    )
    return jax.shard_map(
        functools.partial(on_device, mesh.shape["dp"], mesh.shape["replica"]),
        mesh=mesh,
        in_specs=in_specs,
        out_specs=out_specs,
        check_vma=False,
    )
```

```python
import functools

import jax
import jax.numpy as jnp
from jax import lax
from jax.experimental import pallas as pl
from jax.experimental.pallas import tpu as pltpu
from jax.sharding import PartitionSpec as P

D = 512
HEADS = 4
TILE = 128
CAP = 2
F1 = 1536
LANES = 128
SUB = 8
MESH = pl.DeviceIdType.MESH
F32 = jnp.float32
BF16 = jnp.bfloat16

NT = (((1,), (1,)), ((), ()))
TN = (((0,), (0,)), ((), ()))


def dot(a, b, dims=(((1,), (0,)), ((), ()))):
    return lax.dot_general(a, b, dims, preferred_element_type=F32)


def sigmoid(v):
    return 0.5 * jnp.tanh(0.5 * v) + 0.5


def mean_rows(v):
    return jnp.mean(v, axis=-1, keepdims=True)


def row_norm(v):
    centered = v - mean_rows(v)
    scale = lax.rsqrt(mean_rows(centered * centered) + 1e-05)
    return centered * scale, scale


def norm_back(grad, unit, scale):
    return scale * (grad - mean_rows(grad) - unit * mean_rows(grad * unit))


def fused_kernel(
    n_dp, nx, ny, ev_h, og_h, wi_h, wo_h, ln_h, of_h, tg_h, home, packed, grad_in, grad_out,
    ev, og, wi, wo, ln, of, tg, wib, wob, slope, gate, val, qry, key, wts, wslope, mixed,
    dproj, spread, send, got, parts, core_in, chip, one_in, mid, two_in, z_out, z_in,
    fin_out, fin_in, ld, pk_s, pk_r, c_s, c_r, o_s, o_r, t_s, t_r, z_s, z_r, f_s, f_r,
):
    me = lax.axis_index("dp")
    rep = lax.axis_index("replica")
    nz = n_dp // 2
    n_rep = nx * ny
    core = lax.rem(me, 2)
    z = lax.div(me, 2)
    a = lax.rem(rep, nx)
    b = lax.div(rep, nx)
    other = me + 1 - 2 * core
    holder = lax.rem(z, ny) == b

    def load(i, source, target):
        return pltpu.make_async_copy(source, target, ld.at[i])

    def load_w(n):
        cut = pl.ds(n * D, D)
        return load(2 + n, wi_h.at[:, cut], wi.at[:, cut])

    loads = {
        "ev": load(0, ev_h, ev), "wi0": load_w(0), "wi1": load_w(1), "wi2": load_w(2),
        "ln": load(5, ln_h, ln), "of": load(6, of_h, of), "tg": load(7, tg_h, tg),
        "og": load(1, og_h, og), "wo": load(8, wo_h, wo),
    }
    for copy in loads.values():
        copy.start()

    barrier = pltpu.get_barrier_semaphore()

    @pl.loop(1, n_dp)
    def _(k):
        pl.semaphore_signal(
            barrier, inc=1, device_id=(lax.rem(me + k, n_dp), rep), device_id_type=MESH
        )

    @pl.loop(1, n_rep)
    def _(k):
        pl.semaphore_signal(
            barrier, inc=1, device_id=(me, lax.rem(rep + k, n_rep)), device_id_type=MESH
        )

    def remote(source, target, send_sem, recv_sem, dp, replica):
        return pltpu.make_async_remote_copy(
            src_ref=source, dst_ref=target, send_sem=send_sem, recv_sem=recv_sem,
            device_id=(dp, replica), device_id_type=MESH,
        )

    def wait_all(ref, count, sem):
        part = ref.at[pl.ds(0, count)]
        pltpu.make_async_copy(part, part, sem).wait()

    def core_copy(s):
        return remote(parts.at[1 - core, s], core_in.at[s], c_s.at[s], c_r.at[s], other, rep)

    def line(s, first):
        along_x = (s % 2 == 0) == first
        return (a, nx, lambda q: b * nx + q) if along_x else (b, ny, lambda q: q * nx + a)

    def one_copies(s):
        own, count, rank = line(s, True)
        for k in range(1, count):
            peer = lax.rem(own + k, count)
            block = chip.at[s, :, peer] if s % 2 == 0 else chip.at[s, peer]
            yield peer, lambda slot, block=block, peer=peer: remote(
                block, one_in.at[s, slot], o_s.at[s, peer], o_r.at[s, slot], me, rank(peer)
            )

    def two_copies(s):
        own, count, rank = line(s, False)
        for k in range(1, count):
            peer = lax.rem(own + k, count)
            yield peer, lambda slot, peer=peer: remote(
                mid.at[s, peer], two_in.at[s, slot], t_s.at[s, peer], t_r.at[s, slot],
                me, rank(peer),
            )

    def core_step(s):
        core_copy(s).wait_recv()
        for i in range(ny):
            chip[s, i] = (
                parts[core, s, i].astype(F32) + core_in[s, i].astype(F32)
            ).astype(BF16)
        own = line(s, True)[0]
        for _, copy in one_copies(s):
            copy(own).start()

    def one_step(s):
        own = line(s, True)[0]
        peers = list(one_copies(s))
        for peer, copy in peers:
            copy(peer).wait_recv()
        block = chip[s, :, own] if s % 2 == 0 else chip[s, own]
        total = block.astype(F32)
        for peer, _ in peers:
            total = total + one_in[s, peer].astype(F32)
        mid[s] = total.astype(BF16)
        own = line(s, False)[0]
        for _, copy in two_copies(s):
            copy(own).start()

    def two_step(s):
        own = line(s, False)[0]
        peers = list(two_copies(s))
        for peer, copy in peers:
            copy(peer).wait_recv()
        total = mid[s, own].astype(F32)
        for peer, _ in peers:
            total = total + two_in[s, peer].astype(F32)
        z_out[:, s] = total.reshape(nz // ny, SUB, LANES).astype(BF16)

    rows = lax.broadcasted_iota(jnp.int32, (TILE, 1), 0)
    cols = lax.broadcasted_iota(jnp.int32, (TILE, TILE), 1)
    row2 = lax.broadcasted_iota(jnp.int32, (TILE, TILE), 0)
    low = lax.broadcasted_iota(jnp.int32, (TILE, LANES), 1) < 64
    zero_b = jnp.zeros((TILE, LANES), BF16)
    pair = lax.div(rows, CAP)

    home[TILE:] = jnp.zeros((TILE, D), F32)

    loads["ev"].wait()
    unit, scale = row_norm(ev[...].astype(F32))
    normed = unit.astype(BF16)

    for n in range(0, F1, 256):
        if n % D == 0:
            loads["wi%d" % (n // D)].wait()
        wib[:, n : n + 256] = wi[:, n : n + 256].astype(BF16)
        proj = dot(normed, wib[:, n : n + 256])
        sig = sigmoid(proj)
        act = proj * sig
        slope[:, n : n + 256] = sig + act * (1.0 - sig)
        if n < D:
            gate[:, n : n + 256] = act
        elif n < 2 * D:
            val[:, n - D : n - D + 256] = act.astype(BF16)
        elif n < 2 * D + 256:
            qry[...] = act.astype(BF16)
        else:
            key[...] = act.astype(BF16)

    for name in ("ln", "of", "tg"):
        loads[name].wait()
    ln_row, of_row, tg_row = ln[me], of[me], tg[me]
    users = ln_row.shape[1]
    lanes = lax.broadcasted_iota(jnp.int32, (1, users), 1)
    at_slot = (of_row - TILE) == pair * CAP
    pool_len = jnp.sum(jnp.where(at_slot, ln_row, 0), axis=1, keepdims=True)
    long_len = jnp.broadcast_to(ln_row[:, 0:1], (TILE, 1))
    live_long = rows < long_len
    live_pool = lax.rem(rows, CAP) < pool_len
    live = jnp.concatenate([live_long, live_pool], axis=0)

    for blk in range(2):
        top = blk * TILE
        keep = cols <= row2
        if blk == 0:
            keep = keep & live_long
            size = long_len
        else:
            keep = keep & (lax.div(cols, CAP) == lax.div(row2, CAP)) & live_pool
            size = pool_len
        inv = 1.0 / jnp.maximum(size, 1).astype(F32)
        for h in range(HEADS):
            lane = (h // 2) * LANES
            mine = low if h % 2 == 0 else ~low
            qh = jnp.where(mine, qry[top : top + TILE, lane : lane + LANES], zero_b)
            score = dot(qh, key[top : top + TILE, lane : lane + LANES], NT) * 0.125
            sig = sigmoid(score)
            act = score * sig
            w = jnp.where(keep, act * inv, 0.0).astype(BF16)
            wts[blk * HEADS + h] = w
            wslope[blk * HEADS + h] = jnp.where(
                keep, (sig + act * (1.0 - sig)) * (inv * 0.125), 0.0
            )
            mixed[top : top + TILE, h * LANES : (h + 1) * LANES] = dot(
                w, val[top : top + TILE, h * LANES : (h + 1) * LANES]
            )

    unit_m, scale_m = row_norm(mixed[...])
    hidden = (gate[...] * unit_m).astype(BF16)
    loads["og"].wait()
    grad_live = jnp.where(live, og[...].astype(F32), 0.0)
    grad_b = grad_live.astype(BF16)

    def emit(s, result, first):
        for i in range(result.shape[1] // LANES):
            piece = result[:, i * LANES : (i + 1) * LANES].reshape(
                nz // ny, ny, 2, SUB, LANES
            )
            for c in range(2):
                for g in range(ny):
                    parts[c, s, g, first + i] = (
                        piece[:, g, c].reshape(nz // ny * SUB, LANES).astype(BF16)
                    )

    hidden_t = hidden.T
    for i in range(2):
        emit(3, dot(hidden_t, grad_b[:, i * 256 : i * 256 + 256]), 2 * i)
    pl.semaphore_wait(barrier, n_dp - 1 + n_rep - 1)
    core_copy(3).start()

    loads["wo"].wait()
    wob[...] = wo[...].astype(BF16)
    dhid = dot(grad_b, wob[...], NT).astype(BF16).astype(F32)
    dproj[:, :D] = (dhid * unit_m * slope[:, :D]).astype(BF16)
    dmix = norm_back(dhid * gate[...], unit_m, scale_m).astype(BF16)

    normed_t = normed.T

    def in_part(s):
        for i in range(2):
            n = s * D + i * 256
            emit(s, dot(normed_t, dproj[:, n : n + 256]), 2 * i)
        core_copy(s).start()

    in_part(0)
    core_step(3)

    for blk in range(2):
        top = blk * TILE
        for p in range(HEADS // 2):
            lane = p * LANES
            kk = key[top : top + TILE, lane : lane + LANES]
            qq = qry[top : top + TILE, lane : lane + LANES]
            dq, dk = [], []
            for h in (2 * p, 2 * p + 1):
                dm = dmix[top : top + TILE, h * LANES : (h + 1) * LANES]
                vh = val[top : top + TILE, h * LANES : (h + 1) * LANES]
                w = wts[blk * HEADS + h]
                dw = dot(dm, vh, NT).astype(BF16).astype(F32)
                dv = dot(w, dm, TN).astype(BF16).astype(F32)
                at = D + h * LANES
                dproj[top : top + TILE, at : at + LANES] = (
                    dv * slope[top : top + TILE, at : at + LANES]
                ).astype(BF16)
                ds = (dw * wslope[blk * HEADS + h]).astype(BF16)
                dq.append(dot(ds, kk))
                dk.append(dot(ds, qq, TN))
            for at, pieces in ((2 * D + lane, dq), (2 * D + 256 + lane, dk)):
                both = jnp.where(low, pieces[0], pieces[1]).astype(BF16).astype(F32)
                dproj[top : top + TILE, at : at + LANES] = (
                    both * slope[top : top + TILE, at : at + LANES]
                ).astype(BF16)

    core_step(0)
    in_part(1)
    in_part(2)
    one_step(3)
    core_step(1)

    dnormed = dot(dproj[...], wib[...], NT).astype(BF16).astype(F32)
    grad = norm_back(dnormed, unit, scale) + grad_live
    grad = jnp.where(live, grad, 0.0)
    core_step(2)
    one_step(0)

    to_target = ((tg_row == pair) & (lanes >= 1)).astype(F32).astype(BF16)
    from_slot = at_slot.astype(F32).astype(BF16)
    moves = dot(to_target, from_slot, NT)
    moves = jnp.where(lax.rem(cols, CAP) == lax.rem(row2, CAP), moves, 0.0)
    moved = dot(moves.astype(BF16), grad[TILE:].astype(BF16))
    for i in range(D // LANES):
        spread[pl.ds(i, TILE, stride=D // LANES), :] = moved[:, i * LANES : (i + 1) * LANES]
    send[...] = spread[...].reshape(send.shape).astype(BF16)

    def packed_copy(t):
        return remote(send.at[t], got.at[me], pk_s, pk_r, t, rep)

    @pl.loop(1, n_dp)
    def _(k):
        packed_copy(lax.rem(me + k, n_dp)).start()

    got[me] = send[me]
    home[:TILE] = grad[:TILE]

    two_step(3)
    one_step(1)
    two_step(0)
    one_step(2)
    two_step(1)
    two_step(2)

    nj = nz // ny
    mine = lax.div(z, ny)

    def z_copy(j):
        return remote(
            z_out.at[j], z_in.at[z], z_s, z_r, (j * ny + b) * 2 + core, rep
        )

    @pl.loop(1, nj)
    def _(k):
        z_copy(lax.rem(mine + k, nj)).start()

    @pl.when(jnp.logical_not(holder))
    def _():
        z_copy(mine).start()

    def fin_copy(r):
        return remote(fin_out, fin_in.at[a], f_s.at[r], f_r, me, r)

    @pl.when(holder)
    def _():
        z_in[z] = z_out[mine]
        wait_all(z_in, nz - 1, z_r)
        fin_out[...] = jnp.sum(z_in[...].astype(F32), axis=0).astype(BF16)

        @pl.loop(1, n_rep)
        def _(k):
            fin_copy(lax.rem(rep + k, n_rep)).start()

        fin_in[a] = fin_out[...]

    wait_all(got, n_dp - 1, pk_r)
    spread[...] = got[...].astype(F32).reshape(spread.shape)
    for i in range(D // LANES):
        packed[:, i * LANES : (i + 1) * LANES] = spread[
            pl.ds(i, packed.shape[0], stride=D // LANES), :
        ]

    @pl.when(holder)
    def _():
        wait_all(fin_in, nx - 1, f_r)

    @pl.when(jnp.logical_not(holder))
    def _():
        wait_all(fin_in, nx, f_r)

    for s in range(4):
        for i in range(nx):
            piece = fin_in[i, s].astype(F32)
            if s < 3:
                at = s * D + i * LANES
                grad_in[:, at : at + LANES] = piece
            else:
                grad_out[:, i * LANES : (i + 1) * LANES] = piece

    for s in range(4):
        core_copy(s).wait_send()
        for _, copy in one_copies(s):
            copy(line(s, True)[0]).wait_send()
        for _, copy in two_copies(s):
            copy(line(s, False)[0]).wait_send()
    wait_all(send, n_dp - 1, pk_s)

    @pl.when(holder)
    def _():
        wait_all(z_out, nj - 1, z_s)

        @pl.loop(1, n_rep)
        def _(k):
            fin_copy(lax.rem(rep + k, n_rep)).wait_send()

    @pl.when(jnp.logical_not(holder))
    def _():
        wait_all(z_out, nj, z_s)


def on_device(n_dp, nx, ny, *args):
    nz = n_dp // 2
    deep = nz // ny * SUB
    rows = args[0].shape[0]
    users = args[4].shape
    dma = pltpu.SemaphoreType.DMA
    any_spec = pl.BlockSpec(memory_space=pl.ANY)
    vmem = pl.BlockSpec(memory_space=pltpu.VMEM)
    return pl.pallas_call(
        functools.partial(fused_kernel, n_dp, nx, ny),
        out_shape=(
            jax.ShapeDtypeStruct((rows, D), F32),
            jax.ShapeDtypeStruct((n_dp * CAP, D), F32),
            jax.ShapeDtypeStruct((SUB, F1), F32),
            jax.ShapeDtypeStruct((SUB, D), F32),
        ),
        in_specs=[any_spec] * 7,
        out_specs=(vmem,) * 4,
        scratch_shapes=[
            pltpu.VMEM((rows, D), BF16),
            pltpu.VMEM((rows, D), BF16),
            pltpu.VMEM((D, F1), F32),
            pltpu.VMEM((D, D), F32),
            pltpu.VMEM(users, jnp.int32),
            pltpu.VMEM(users, jnp.int32),
            pltpu.VMEM(users, jnp.int32),
            pltpu.VMEM((D, F1), BF16),
            pltpu.VMEM((D, D), BF16),
            pltpu.VMEM((rows, F1), F32),
            pltpu.VMEM((rows, D), F32),
            pltpu.VMEM((rows, D), BF16),
            pltpu.VMEM((rows, 256), BF16),
            pltpu.VMEM((rows, 256), BF16),
            pltpu.VMEM((2 * HEADS, TILE, TILE), BF16),
            pltpu.VMEM((2 * HEADS, TILE, TILE), F32),
            pltpu.VMEM((rows, D), F32),
            pltpu.VMEM((rows, F1), BF16),
            pltpu.VMEM((TILE * D // LANES, LANES), F32),
            pltpu.VMEM((n_dp, SUB, LANES), BF16),
            pltpu.VMEM((n_dp, SUB, LANES), BF16),
            pltpu.VMEM((2, 4, ny, nx, deep, LANES), BF16),
            pltpu.VMEM((4, ny, nx, deep, LANES), BF16),
            pltpu.VMEM((4, ny, nx, deep, LANES), BF16),
            pltpu.VMEM((4, nx, ny, deep, LANES), BF16),
            pltpu.VMEM((4, nx, deep, LANES), BF16),
            pltpu.VMEM((4, nx, deep, LANES), BF16),
            pltpu.VMEM((nz // ny, 4, SUB, LANES), BF16),
            pltpu.VMEM((nz, 4, SUB, LANES), BF16),
            pltpu.VMEM((4, SUB, LANES), BF16),
            pltpu.VMEM((nx, 4, SUB, LANES), BF16),
            dma((9,)),
            dma, dma,
            dma((4,)), dma((4,)),
            dma((4, nx)), dma((4, nx)),
            dma((4, nx)), dma((4, nx)),
            dma, dma,
            dma((nx * ny,)), dma,
        ],
        compiler_params=pltpu.CompilerParams(
            collective_id=0, has_side_effects=True, vmem_limit_bytes=56 * 2**20
        ),
        name="fused",
    )(*args)


def solution(mesh):
    in_specs = (
        P(("dp", "replica"), None),
        P(("dp", "replica"), None),
        P(),
        P(),
        P(None, "replica", None),
        P(None, "replica", None),
        P(None, "replica", None),
    )
    out_specs = (
        P(("dp", "replica"), None),
        P(("dp", "replica"), None),
        P("dp", None),
        P("dp", None),
    )
    return jax.shard_map(
        functools.partial(on_device, mesh.shape["dp"], 4, mesh.shape["replica"] // 4),
        mesh=mesh,
        in_specs=in_specs,
        out_specs=out_specs,
        check_vma=False,
    )
```

```python
import functools

import jax
import jax.numpy as jnp
from jax import lax
from jax.experimental import pallas as pl
from jax.experimental.pallas import tpu as pltpu
from jax.sharding import PartitionSpec as P

D = 512
HEADS = 4
TILE = 128
CAP = 2
F1 = 1536
LANES = 128
SUB = 8
MESH = pl.DeviceIdType.MESH
F32 = jnp.float32
BF16 = jnp.bfloat16

NT = (((1,), (1,)), ((), ()))
TN = (((0,), (0,)), ((), ()))


def dot(a, b, dims=(((1,), (0,)), ((), ()))):
    return lax.dot_general(a, b, dims, preferred_element_type=F32)


def sigmoid(v):
    return 0.5 * jnp.tanh(0.5 * v) + 0.5


def mean_rows(v):
    return jnp.mean(v, axis=-1, keepdims=True)


def row_norm(v):
    centered = v - mean_rows(v)
    scale = lax.rsqrt(mean_rows(centered * centered) + 1e-05)
    return centered * scale, scale


def norm_back(grad, unit, scale):
    return scale * (grad - mean_rows(grad) - unit * mean_rows(grad * unit))


def fused_kernel(
    n_dp, nx, ny, ev_h, og_h, wi_h, wo_h, ln_h, of_h, tg_h, home, packed, grad_in, grad_out,
    ev, og, wi, wo, ln, of, tg, wib, wob, slope, gate, val, qry, key, wts, wslope, mixed,
    dproj, spread, send, got, parts, core_in, chip, one_in, mid, two_in, z_out, z_in,
    fin_out, fin_in, ld, pk_s, pk_r, c_s, c_r, o_s, o_r, t_s, t_r, z_s, z_r, f_s, f_r,
):
    me = lax.axis_index("dp")
    rep = lax.axis_index("replica")
    nz = n_dp // 2
    n_rep = nx * ny
    core = lax.rem(me, 2)
    z = lax.div(me, 2)
    a = lax.rem(rep, nx)
    b = lax.div(rep, nx)
    other = me + 1 - 2 * core
    holder = lax.rem(z, ny) == b

    def load(i, source, target):
        return pltpu.make_async_copy(source, target, ld.at[i])

    def load_w(n):
        cut = pl.ds(n * D, D)
        return load(2 + n, wi_h.at[:, cut], wi.at[:, cut])

    loads = {
        "ev": load(0, ev_h, ev), "wi0": load_w(0), "wi1": load_w(1), "wi2": load_w(2),
        "ln": load(5, ln_h, ln), "of": load(6, of_h, of), "tg": load(7, tg_h, tg),
        "og": load(1, og_h, og), "wo": load(8, wo_h, wo),
    }
    for copy in loads.values():
        copy.start()

    barrier = pltpu.get_barrier_semaphore()

    def farthest(i, count):
        step = lax.div(i + 1, 2)
        return count // 2 + step * (2 * lax.rem(i + 1, 2) - 1)

    @pl.loop(0, n_dp - 1)
    def _(i):
        peer = lax.rem(me + farthest(i, n_dp), n_dp)
        pl.semaphore_signal(
            barrier, inc=1, device_id=(peer, rep), device_id_type=MESH
        )

    @pl.loop(1, n_rep)
    def _(k):
        pl.semaphore_signal(
            barrier, inc=1, device_id=(me, lax.rem(rep + k, n_rep)), device_id_type=MESH
        )

    def remote(source, target, send_sem, recv_sem, dp, replica):
        return pltpu.make_async_remote_copy(
            src_ref=source, dst_ref=target, send_sem=send_sem, recv_sem=recv_sem,
            device_id=(dp, replica), device_id_type=MESH,
        )

    def wait_all(ref, count, sem):
        part = ref.at[pl.ds(0, count)]
        pltpu.make_async_copy(part, part, sem).wait()

    def core_copy(s):
        return remote(parts.at[1 - core, s], core_in.at[s], c_s.at[s], c_r.at[s], other, rep)

    def line(s, first):
        along_x = (s % 2 == 0) == first
        return (a, nx, lambda q: b * nx + q) if along_x else (b, ny, lambda q: q * nx + a)

    def one_copies(s):
        own, count, rank = line(s, True)
        for k in range(1, count):
            peer = lax.rem(own + k, count)
            block = chip.at[s, :, peer] if s % 2 == 0 else chip.at[s, peer]
            yield peer, lambda slot, block=block, peer=peer: remote(
                block, one_in.at[s, slot], o_s.at[s, peer], o_r.at[s, slot], me, rank(peer)
            )

    def two_copies(s):
        own, count, rank = line(s, False)
        for k in range(1, count):
            peer = lax.rem(own + k, count)
            yield peer, lambda slot, peer=peer: remote(
                mid.at[s, peer], two_in.at[s, slot], t_s.at[s, peer], t_r.at[s, slot],
                me, rank(peer),
            )

    def core_step(s):
        core_copy(s).wait_recv()
        for i in range(ny):
            chip[s, i] = (
                parts[core, s, i].astype(F32) + core_in[s, i].astype(F32)
            ).astype(BF16)
        own = line(s, True)[0]
        for _, copy in one_copies(s):
            copy(own).start()

    def one_step(s):
        own = line(s, True)[0]
        peers = list(one_copies(s))
        for peer, copy in peers:
            copy(peer).wait_recv()
        block = chip[s, :, own] if s % 2 == 0 else chip[s, own]
        total = block.astype(F32)
        for peer, _ in peers:
            total = total + one_in[s, peer].astype(F32)
        mid[s] = total.astype(BF16)
        own = line(s, False)[0]
        for _, copy in two_copies(s):
            copy(own).start()

    def two_step(s):
        own = line(s, False)[0]
        peers = list(two_copies(s))
        for peer, copy in peers:
            copy(peer).wait_recv()
        total = mid[s, own].astype(F32)
        for peer, _ in peers:
            total = total + two_in[s, peer].astype(F32)
        z_out[:, s] = total.reshape(nz // ny, SUB, LANES).astype(BF16)

    rows = lax.broadcasted_iota(jnp.int32, (TILE, 1), 0)
    cols = lax.broadcasted_iota(jnp.int32, (TILE, TILE), 1)
    row2 = lax.broadcasted_iota(jnp.int32, (TILE, TILE), 0)
    low = lax.broadcasted_iota(jnp.int32, (TILE, LANES), 1) < 64
    zero_b = jnp.zeros((TILE, LANES), BF16)
    pair = lax.div(rows, CAP)

    loads["ev"].wait()
    unit, scale = row_norm(ev[...].astype(F32))
    normed = unit.astype(BF16)

    for n in range(0, F1, 256):
        if n % D == 0:
            loads["wi%d" % (n // D)].wait()
        wib[:, n : n + 256] = wi[:, n : n + 256].astype(BF16)
        proj = dot(normed, wib[:, n : n + 256])
        sig = sigmoid(proj)
        act = proj * sig
        slope[:, n : n + 256] = sig + act * (1.0 - sig)
        if n < D:
            gate[:, n : n + 256] = act
        elif n < 2 * D:
            val[:, n - D : n - D + 256] = act.astype(BF16)
        elif n < 2 * D + 256:
            qry[...] = act.astype(BF16)
        else:
            key[...] = act.astype(BF16)

    for name in ("ln", "of", "tg"):
        loads[name].wait()
    ln_row, of_row, tg_row = ln[me], of[me], tg[me]
    users = ln_row.shape[1]
    lanes = lax.broadcasted_iota(jnp.int32, (1, users), 1)
    at_slot = (of_row - TILE) == pair * CAP
    pool_len = jnp.sum(jnp.where(at_slot, ln_row, 0), axis=1, keepdims=True)
    long_len = jnp.broadcast_to(ln_row[:, 0:1], (TILE, 1))
    live_long = rows < long_len
    live_pool = lax.rem(rows, CAP) < pool_len
    live = jnp.concatenate([live_long, live_pool], axis=0)

    for blk in range(2):
        top = blk * TILE
        keep = cols <= row2
        if blk == 0:
            keep = keep & live_long
            size = long_len
        else:
            keep = keep & (lax.div(cols, CAP) == lax.div(row2, CAP)) & live_pool
            size = pool_len
        inv = 1.0 / jnp.maximum(size, 1).astype(F32)
        for h in range(HEADS):
            lane = (h // 2) * LANES
            mine = low if h % 2 == 0 else ~low
            qh = jnp.where(mine, qry[top : top + TILE, lane : lane + LANES], zero_b)
            score = dot(qh, key[top : top + TILE, lane : lane + LANES], NT) * 0.125
            sig = sigmoid(score)
            act = score * sig
            w = jnp.where(keep, act * inv, 0.0).astype(BF16)
            wts[blk * HEADS + h] = w
            wslope[blk * HEADS + h] = jnp.where(
                keep, (sig + act * (1.0 - sig)) * (inv * 0.125), 0.0
            )
            mixed[top : top + TILE, h * LANES : (h + 1) * LANES] = dot(
                w, val[top : top + TILE, h * LANES : (h + 1) * LANES]
            )

    unit_m, scale_m = row_norm(mixed[...])
    hidden = (gate[...] * unit_m).astype(BF16)
    loads["og"].wait()
    grad_live = jnp.where(live, og[...].astype(F32), 0.0)
    grad_b = grad_live.astype(BF16)

    def emit(s, result, first):
        for i in range(result.shape[1] // LANES):
            piece = result[:, i * LANES : (i + 1) * LANES].reshape(
                nz // ny, ny, 2, SUB, LANES
            )
            for c in range(2):
                for g in range(ny):
                    parts[c, s, g, first + i] = (
                        piece[:, g, c].reshape(nz // ny * SUB, LANES).astype(BF16)
                    )

    hidden_t = hidden.T
    for i in range(2):
        emit(3, dot(hidden_t, grad_b[:, i * 256 : i * 256 + 256]), 2 * i)

    loads["wo"].wait()
    wob[...] = wo[...].astype(BF16)
    dhid = dot(grad_b, wob[...], NT).astype(BF16).astype(F32)
    dproj[:, :D] = (dhid * unit_m * slope[:, :D]).astype(BF16)
    dmix = norm_back(dhid * gate[...], unit_m, scale_m).astype(BF16)

    normed_t = normed.T

    def in_part(s):
        for i in range(2):
            n = s * D + i * 256
            emit(s, dot(normed_t, dproj[:, n : n + 256]), 2 * i)

    in_part(0)

    for blk in range(2):
        top = blk * TILE
        for p in range(HEADS // 2):
            lane = p * LANES
            kk = key[top : top + TILE, lane : lane + LANES]
            qq = qry[top : top + TILE, lane : lane + LANES]
            dq, dk = [], []
            for h in (2 * p, 2 * p + 1):
                dm = dmix[top : top + TILE, h * LANES : (h + 1) * LANES]
                vh = val[top : top + TILE, h * LANES : (h + 1) * LANES]
                w = wts[blk * HEADS + h]
                dw = dot(dm, vh, NT).astype(BF16).astype(F32)
                dv = dot(w, dm, TN).astype(BF16).astype(F32)
                at = D + h * LANES
                dproj[top : top + TILE, at : at + LANES] = (
                    dv * slope[top : top + TILE, at : at + LANES]
                ).astype(BF16)
                ds = (dw * wslope[blk * HEADS + h]).astype(BF16)
                dq.append(dot(ds, kk))
                dk.append(dot(ds, qq, TN))
            for at, pieces in ((2 * D + lane, dq), (2 * D + 256 + lane, dk)):
                both = jnp.where(low, pieces[0], pieces[1]).astype(BF16).astype(F32)
                dproj[top : top + TILE, at : at + LANES] = (
                    both * slope[top : top + TILE, at : at + LANES]
                ).astype(BF16)

    in_part(1)
    in_part(2)

    dnormed = dot(dproj[...], wib[...], NT).astype(BF16).astype(F32)
    grad = norm_back(dnormed, unit, scale) + grad_live
    grad = jnp.where(live, grad, 0.0)

    to_target = ((tg_row == pair) & (lanes >= 1)).astype(F32).astype(BF16)
    from_slot = at_slot.astype(F32).astype(BF16)
    moves = dot(to_target, from_slot, NT)
    moves = jnp.where(lax.rem(cols, CAP) == lax.rem(row2, CAP), moves, 0.0)
    moved = dot(moves.astype(BF16), grad[TILE:].astype(BF16))
    for i in range(D // LANES):
        spread[pl.ds(i, TILE, stride=D // LANES), :] = moved[:, i * LANES : (i + 1) * LANES]
    send[...] = spread[...].reshape(send.shape).astype(BF16)

    pl.semaphore_wait(barrier, n_dp - 1 + n_rep - 1)
    for s in (3, 0, 1, 2):
        core_copy(s).start()

    def packed_copy(t):
        return remote(send.at[t], got.at[me], pk_s, pk_r, t, rep)

    @pl.loop(0, n_dp - 1)
    def _(i):
        packed_copy(lax.rem(me + farthest(i, n_dp), n_dp)).start()

    got[me] = send[me]
    home[...] = grad[:TILE]

    core_step(3)
    core_step(0)
    core_step(1)
    one_step(3)
    core_step(2)
    one_step(0)
    two_step(3)
    one_step(1)
    two_step(0)
    one_step(2)
    two_step(1)
    two_step(2)

    nj = nz // ny
    mine = lax.div(z, ny)

    def z_copy(j):
        return remote(
            z_out.at[j], z_in.at[z], z_s, z_r, (j * ny + b) * 2 + core, rep
        )

    @pl.loop(0, nj - 1)
    def _(i):
        z_copy(lax.rem(mine + farthest(i, nj), nj)).start()

    @pl.when(jnp.logical_not(holder))
    def _():
        z_copy(mine).start()

    def fin_copy(r):
        return remote(fin_out, fin_in.at[a], f_s.at[r], f_r, me, r)

    @pl.when(holder)
    def _():
        z_in[z] = z_out[mine]
        wait_all(z_in, nz - 1, z_r)
        fin_out[...] = jnp.sum(z_in[...].astype(F32), axis=0).astype(BF16)

        @pl.loop(1, n_rep)
        def _(k):
            fin_copy(lax.rem(rep + k, n_rep)).start()

        fin_in[a] = fin_out[...]

    wait_all(got, n_dp - 1, pk_r)
    spread[...] = got[...].astype(F32).reshape(spread.shape)
    for i in range(D // LANES):
        packed[:, i * LANES : (i + 1) * LANES] = spread[
            pl.ds(i, packed.shape[0], stride=D // LANES), :
        ]

    @pl.when(holder)
    def _():
        wait_all(fin_in, nx - 1, f_r)

    @pl.when(jnp.logical_not(holder))
    def _():
        wait_all(fin_in, nx, f_r)

    for s in range(4):
        for i in range(nx):
            piece = fin_in[i, s].astype(F32)
            if s < 3:
                at = s * D + i * LANES
                grad_in[:, at : at + LANES] = piece
            else:
                grad_out[:, i * LANES : (i + 1) * LANES] = piece

    for s in range(4):
        core_copy(s).wait_send()
        for _, copy in one_copies(s):
            copy(line(s, True)[0]).wait_send()
        for _, copy in two_copies(s):
            copy(line(s, False)[0]).wait_send()
    wait_all(send, n_dp - 1, pk_s)

    @pl.when(holder)
    def _():
        wait_all(z_out, nj - 1, z_s)

        @pl.loop(1, n_rep)
        def _(k):
            fin_copy(lax.rem(rep + k, n_rep)).wait_send()

    @pl.when(jnp.logical_not(holder))
    def _():
        wait_all(z_out, nj, z_s)


def place_kernel(*refs):
    count = (len(refs) - 3) // 3
    sources, targets, held = refs[:count], refs[count : 2 * count], refs[2 * count : -3]
    zero, inward, outward = refs[-3:]
    top = sources[0].shape[0]
    here = [
        pltpu.make_async_copy(sources[i], held[i], inward.at[i]) for i in range(count)
    ]
    there = [
        pltpu.make_async_copy(
            held[i], targets[i].at[pl.ds(0, top)] if i == 0 else targets[i], outward.at[i]
        )
        for i in range(count)
    ]
    for copy in here:
        copy.start()
    zero[...] = jnp.zeros_like(zero)
    rest = pltpu.make_async_copy(
        zero, targets[0].at[pl.ds(top, zero.shape[0])], outward.at[count]
    )
    rest.start()
    for i in range(count):
        here[i].wait()
        there[i].start()
    for copy in there:
        copy.wait()
    rest.wait()


def place(home_rows, *results):
    top = results[0].shape[0]
    hbm = pl.BlockSpec(memory_space=pltpu.HBM)
    return pl.pallas_call(
        place_kernel,
        out_shape=(jax.ShapeDtypeStruct((home_rows, D), F32),)
        + tuple(jax.ShapeDtypeStruct(v.shape, v.dtype) for v in results[1:]),
        in_specs=[hbm] * 4,
        out_specs=(hbm,) * 4,
        scratch_shapes=[pltpu.VMEM(v.shape, v.dtype) for v in results]
        + [
            pltpu.VMEM((home_rows - top, D), F32),
            pltpu.SemaphoreType.DMA((4,)),
            pltpu.SemaphoreType.DMA((5,)),
        ],
        name="place",
    )(*results)


def on_device(n_dp, nx, ny, *args):
    nz = n_dp // 2
    deep = nz // ny * SUB
    rows = args[0].shape[0]
    users = args[4].shape
    dma = pltpu.SemaphoreType.DMA
    any_spec = pl.BlockSpec(memory_space=pltpu.HBM)
    vmem = pl.BlockSpec(memory_space=pltpu.VMEM)
    results = pl.pallas_call(
        functools.partial(fused_kernel, n_dp, nx, ny),
        out_shape=(
            jax.ShapeDtypeStruct((TILE, D), F32),
            jax.ShapeDtypeStruct((n_dp * CAP, D), F32),
            jax.ShapeDtypeStruct((SUB, F1), F32),
            jax.ShapeDtypeStruct((SUB, D), F32),
        ),
        in_specs=[any_spec] * 7,
        out_specs=(vmem,) * 4,
        scratch_shapes=[
            pltpu.VMEM((rows, D), BF16),
            pltpu.VMEM((rows, D), BF16),
            pltpu.VMEM((D, F1), F32),
            pltpu.VMEM((D, D), F32),
            pltpu.VMEM(users, jnp.int32),
            pltpu.VMEM(users, jnp.int32),
            pltpu.VMEM(users, jnp.int32),
            pltpu.VMEM((D, F1), BF16),
            pltpu.VMEM((D, D), BF16),
            pltpu.VMEM((rows, F1), F32),
            pltpu.VMEM((rows, D), F32),
            pltpu.VMEM((rows, D), BF16),
            pltpu.VMEM((rows, 256), BF16),
            pltpu.VMEM((rows, 256), BF16),
            pltpu.VMEM((2 * HEADS, TILE, TILE), BF16),
            pltpu.VMEM((2 * HEADS, TILE, TILE), F32),
            pltpu.VMEM((rows, D), F32),
            pltpu.VMEM((rows, F1), BF16),
            pltpu.VMEM((TILE * D // LANES, LANES), F32),
            pltpu.VMEM((n_dp, SUB, LANES), BF16),
            pltpu.VMEM((n_dp, SUB, LANES), BF16),
            pltpu.VMEM((2, 4, ny, nx, deep, LANES), BF16),
            pltpu.VMEM((4, ny, nx, deep, LANES), BF16),
            pltpu.VMEM((4, ny, nx, deep, LANES), BF16),
            pltpu.VMEM((4, nx, ny, deep, LANES), BF16),
            pltpu.VMEM((4, nx, deep, LANES), BF16),
            pltpu.VMEM((4, nx, deep, LANES), BF16),
            pltpu.VMEM((nz // ny, 4, SUB, LANES), BF16),
            pltpu.VMEM((nz, 4, SUB, LANES), BF16),
            pltpu.VMEM((4, SUB, LANES), BF16),
            pltpu.VMEM((nx, 4, SUB, LANES), BF16),
            dma((9,)),
            dma, dma,
            dma((4,)), dma((4,)),
            dma((4, nx)), dma((4, nx)),
            dma((4, nx)), dma((4, nx)),
            dma, dma,
            dma((nx * ny,)), dma,
        ],
        compiler_params=pltpu.CompilerParams(
            collective_id=0, has_side_effects=True, vmem_limit_bytes=58 * 2**20
        ),
        name="fused",
    )(*args)
    return place(rows, *results)


def solution(mesh):
    in_specs = (
        P(("dp", "replica"), None),
        P(("dp", "replica"), None),
        P(),
        P(),
        P(None, "replica", None),
        P(None, "replica", None),
        P(None, "replica", None),
    )
    out_specs = (
        P(("dp", "replica"), None),
        P(("dp", "replica"), None),
        P("dp", None),
        P("dp", None),
    )
    return jax.shard_map(
        functools.partial(on_device, mesh.shape["dp"], 4, mesh.shape["replica"] // 4),
        mesh=mesh,
        in_specs=in_specs,
        out_specs=out_specs,
        check_vma=False,
    )
```

```python
import functools

import jax
import jax.numpy as jnp
from jax import lax
from jax.experimental import pallas as pl
from jax.experimental.pallas import tpu as pltpu
from jax.sharding import PartitionSpec as P

D = 512
HEADS = 4
TILE = 128
CAP = 2
F1 = 1536
LANES = 128
SUB = 8
MESH = pl.DeviceIdType.MESH
F32 = jnp.float32
BF16 = jnp.bfloat16

NT = (((1,), (1,)), ((), ()))
TN = (((0,), (0,)), ((), ()))


def dot(a, b, dims=(((1,), (0,)), ((), ()))):
    return lax.dot_general(a, b, dims, preferred_element_type=F32)


def sigmoid(v):
    return 0.5 * jnp.tanh(0.5 * v) + 0.5


def mean_rows(v):
    return jnp.mean(v, axis=-1, keepdims=True)


def row_norm(v):
    centered = v - mean_rows(v)
    scale = lax.rsqrt(mean_rows(centered * centered) + 1e-05)
    return centered * scale, scale


def norm_back(grad, unit, scale):
    return scale * (grad - mean_rows(grad) - unit * mean_rows(grad * unit))


def fused_kernel(
    n_dp, nx, ny, ev_h, og_h, wi_h, wo_h, ln_h, of_h, tg_h, home, packed, grad_in, grad_out,
    ev, og, wi, wo, ln, of, tg, wib, wob, slope, gate, val, qry, key, wts, wslope, mixed,
    dproj, spread, send, got, parts, core_in, chip, one_in, mid, two_in, z_out, z_in,
    fin_out, fin_in, ld, pk_s, pk_r, c_s, c_r, o_s, o_r, t_s, t_r, z_s, z_r, f_s, f_r, far_sem,
):
    me = lax.axis_index("dp")
    rep = lax.axis_index("replica")
    nz = n_dp // 2
    n_rep = nx * ny
    core = lax.rem(me, 2)
    z = lax.div(me, 2)
    a = lax.rem(rep, nx)
    b = lax.div(rep, nx)
    other = me + 1 - 2 * core
    holder = lax.rem(z, ny) == b

    def load(i, source, target):
        return pltpu.make_async_copy(source, target, ld.at[i])

    def load_w(n):
        cut = pl.ds(n * D, D)
        return load(2 + n, wi_h.at[:, cut], wi.at[:, cut])

    loads = {
        "ev": load(0, ev_h, ev), "wi0": load_w(0), "wi1": load_w(1), "wi2": load_w(2),
        "ln": load(5, ln_h, ln), "of": load(6, of_h, of), "tg": load(7, tg_h, tg),
        "og": load(1, og_h, og), "wo": load(8, wo_h, wo),
    }
    for copy in loads.values():
        copy.start()

    barrier = pltpu.get_barrier_semaphore()

    def farthest(i, count):
        step = lax.div(i + 1, 2)
        return count // 2 + step * (2 * lax.rem(i + 1, 2) - 1)

    jump = n_dp // 4

    @pl.loop(0, jump + 1)
    def _(i):
        for away in (jump + 1 - i, n_dp - jump - 1 + i):
            pl.semaphore_signal(
                barrier, inc=1, device_id=(lax.rem(me + away, n_dp), rep),
                device_id_type=MESH,
            )

    @pl.loop(1, n_rep)
    def _(k):
        pl.semaphore_signal(
            barrier, inc=1, device_id=(me, lax.rem(rep + k, n_rep)), device_id_type=MESH
        )

    def remote(source, target, send_sem, recv_sem, dp, replica):
        return pltpu.make_async_remote_copy(
            src_ref=source, dst_ref=target, send_sem=send_sem, recv_sem=recv_sem,
            device_id=(dp, replica), device_id_type=MESH,
        )

    def wait_all(ref, count, sem):
        part = ref.at[pl.ds(0, count)]
        pltpu.make_async_copy(part, part, sem).wait()

    def core_copy(s):
        return remote(parts.at[1 - core, s], core_in.at[s], c_s.at[s], c_r.at[s], other, rep)

    def line(s, first):
        along_x = (s % 2 == 0) == first
        return (a, nx, lambda q: b * nx + q) if along_x else (b, ny, lambda q: q * nx + a)

    def one_copies(s):
        own, count, rank = line(s, True)
        for k in range(1, count):
            peer = lax.rem(own + k, count)
            block = chip.at[s, :, peer] if s % 2 == 0 else chip.at[s, peer]
            yield peer, lambda slot, block=block, peer=peer: remote(
                block, one_in.at[s, slot], o_s.at[s, peer], o_r.at[s, slot], me, rank(peer)
            )

    def two_copies(s):
        own, count, rank = line(s, False)
        for k in range(1, count):
            peer = lax.rem(own + k, count)
            yield peer, lambda slot, peer=peer: remote(
                mid.at[s, peer], two_in.at[s, slot], t_s.at[s, peer], t_r.at[s, slot],
                me, rank(peer),
            )

    def core_step(s):
        core_copy(s).wait_recv()
        for i in range(ny):
            chip[s, i] = (
                parts[core, s, i].astype(F32) + core_in[s, i].astype(F32)
            ).astype(BF16)
        own = line(s, True)[0]
        for _, copy in one_copies(s):
            copy(own).start()

    def one_step(s):
        own = line(s, True)[0]
        peers = list(one_copies(s))
        for peer, copy in peers:
            copy(peer).wait_recv()
        block = chip[s, :, own] if s % 2 == 0 else chip[s, own]
        total = block.astype(F32)
        for peer, _ in peers:
            total = total + one_in[s, peer].astype(F32)
        mid[s] = total.astype(BF16)
        own = line(s, False)[0]
        for _, copy in two_copies(s):
            copy(own).start()

    def two_step(s):
        own = line(s, False)[0]
        peers = list(two_copies(s))
        for peer, copy in peers:
            copy(peer).wait_recv()
        total = mid[s, own].astype(F32)
        for peer, _ in peers:
            total = total + two_in[s, peer].astype(F32)
        z_out[:, s] = total.reshape(nz // ny, SUB, LANES).astype(BF16)

    rows = lax.broadcasted_iota(jnp.int32, (TILE, 1), 0)
    cols = lax.broadcasted_iota(jnp.int32, (TILE, TILE), 1)
    row2 = lax.broadcasted_iota(jnp.int32, (TILE, TILE), 0)
    low = lax.broadcasted_iota(jnp.int32, (TILE, LANES), 1) < 64
    zero_b = jnp.zeros((TILE, LANES), BF16)
    pair = lax.div(rows, CAP)

    loads["ev"].wait()
    unit, scale = row_norm(ev[...].astype(F32))
    normed = unit.astype(BF16)

    for n in range(0, F1, 256):
        if n % D == 0:
            loads["wi%d" % (n // D)].wait()
        wib[:, n : n + 256] = wi[:, n : n + 256].astype(BF16)
        proj = dot(normed, wib[:, n : n + 256])
        sig = sigmoid(proj)
        act = proj * sig
        slope[:, n : n + 256] = sig + act * (1.0 - sig)
        if n < D:
            gate[:, n : n + 256] = act
        elif n < 2 * D:
            val[:, n - D : n - D + 256] = act.astype(BF16)
        elif n < 2 * D + 256:
            qry[...] = act.astype(BF16)
        else:
            key[...] = act.astype(BF16)

    for name in ("ln", "of", "tg"):
        loads[name].wait()
    ln_row, of_row, tg_row = ln[me], of[me], tg[me]
    users = ln_row.shape[1]
    lanes = lax.broadcasted_iota(jnp.int32, (1, users), 1)
    at_slot = (of_row - TILE) == pair * CAP
    pool_len = jnp.sum(jnp.where(at_slot, ln_row, 0), axis=1, keepdims=True)
    long_len = jnp.broadcast_to(ln_row[:, 0:1], (TILE, 1))
    live_long = rows < long_len
    live_pool = lax.rem(rows, CAP) < pool_len
    live = jnp.concatenate([live_long, live_pool], axis=0)

    for blk in range(2):
        top = blk * TILE
        keep = cols <= row2
        if blk == 0:
            keep = keep & live_long
            size = long_len
        else:
            keep = keep & (lax.div(cols, CAP) == lax.div(row2, CAP)) & live_pool
            size = pool_len
        inv = 1.0 / jnp.maximum(size, 1).astype(F32)
        for h in range(HEADS):
            lane = (h // 2) * LANES
            mine = low if h % 2 == 0 else ~low
            qh = jnp.where(mine, qry[top : top + TILE, lane : lane + LANES], zero_b)
            score = dot(qh, key[top : top + TILE, lane : lane + LANES], NT) * 0.125
            sig = sigmoid(score)
            act = score * sig
            w = jnp.where(keep, act * inv, 0.0).astype(BF16)
            wts[blk * HEADS + h] = w
            wslope[blk * HEADS + h] = jnp.where(
                keep, (sig + act * (1.0 - sig)) * (inv * 0.125), 0.0
            )
            mixed[top : top + TILE, h * LANES : (h + 1) * LANES] = dot(
                w, val[top : top + TILE, h * LANES : (h + 1) * LANES]
            )

    unit_m, scale_m = row_norm(mixed[...])
    hidden = (gate[...] * unit_m).astype(BF16)
    loads["og"].wait()
    grad_live = jnp.where(live, og[...].astype(F32), 0.0)
    grad_b = grad_live.astype(BF16)

    def emit(s, result, first):
        for i in range(result.shape[1] // LANES):
            piece = result[:, i * LANES : (i + 1) * LANES].reshape(
                nz // ny, ny, 2, SUB, LANES
            )
            for c in range(2):
                for g in range(ny):
                    parts[c, s, g, first + i] = (
                        piece[:, g, c].reshape(nz // ny * SUB, LANES).astype(BF16)
                    )

    hidden_t = hidden.T
    for i in range(2):
        emit(3, dot(hidden_t, grad_b[:, i * 256 : i * 256 + 256]), 2 * i)
    pl.semaphore_wait(barrier, 2 * (jump + 1) + n_rep - 1)
    for away in (jump, n_dp - jump):
        pl.semaphore_signal(
            far_sem, inc=1, device_id=(lax.rem(me + away, n_dp), rep), device_id_type=MESH
        )

    core_copy(3).start()

    loads["wo"].wait()
    wob[...] = wo[...].astype(BF16)
    dhid = dot(grad_b, wob[...], NT).astype(BF16).astype(F32)
    dproj[:, :D] = (dhid * unit_m * slope[:, :D]).astype(BF16)
    dmix = norm_back(dhid * gate[...], unit_m, scale_m).astype(BF16)

    normed_t = normed.T

    def in_part(s):
        for i in range(2):
            n = s * D + i * 256
            emit(s, dot(normed_t, dproj[:, n : n + 256]), 2 * i)
        core_copy(s).start()

    in_part(0)

    for blk in range(2):
        top = blk * TILE
        for p in range(HEADS // 2):
            lane = p * LANES
            kk = key[top : top + TILE, lane : lane + LANES]
            qq = qry[top : top + TILE, lane : lane + LANES]
            dq, dk = [], []
            for h in (2 * p, 2 * p + 1):
                dm = dmix[top : top + TILE, h * LANES : (h + 1) * LANES]
                vh = val[top : top + TILE, h * LANES : (h + 1) * LANES]
                w = wts[blk * HEADS + h]
                dw = dot(dm, vh, NT).astype(BF16).astype(F32)
                dv = dot(w, dm, TN).astype(BF16).astype(F32)
                at = D + h * LANES
                dproj[top : top + TILE, at : at + LANES] = (
                    dv * slope[top : top + TILE, at : at + LANES]
                ).astype(BF16)
                ds = (dw * wslope[blk * HEADS + h]).astype(BF16)
                dq.append(dot(ds, kk))
                dk.append(dot(ds, qq, TN))
            for at, pieces in ((2 * D + lane, dq), (2 * D + 256 + lane, dk)):
                both = jnp.where(low, pieces[0], pieces[1]).astype(BF16).astype(F32)
                dproj[top : top + TILE, at : at + LANES] = (
                    both * slope[top : top + TILE, at : at + LANES]
                ).astype(BF16)

    core_step(3)
    core_step(0)
    in_part(1)
    in_part(2)

    dnormed = dot(dproj[...], wib[...], NT).astype(BF16).astype(F32)
    grad = norm_back(dnormed, unit, scale) + grad_live
    grad = jnp.where(live, grad, 0.0)

    to_target = ((tg_row == pair) & (lanes >= 1)).astype(F32).astype(BF16)
    from_slot = at_slot.astype(F32).astype(BF16)
    moves = dot(to_target, from_slot, NT)
    moves = jnp.where(lax.rem(cols, CAP) == lax.rem(row2, CAP), moves, 0.0)
    moved = dot(moves.astype(BF16), grad[TILE:].astype(BF16))
    for i in range(D // LANES):
        spread[pl.ds(i, TILE, stride=D // LANES), :] = moved[:, i * LANES : (i + 1) * LANES]
    send[...] = spread[...].reshape(send.shape).astype(BF16)

    def packed_copy(t):
        return remote(send.at[t], got.at[me], pk_s, pk_r, t, rep)

    core_step(1)
    core_step(2)

    pl.semaphore_wait(far_sem, 2)

    @pl.loop(0, n_dp - 1)
    def _(i):
        packed_copy(lax.rem(me + farthest(i, n_dp), n_dp)).start()

    got[me] = send[me]
    home[...] = grad[:TILE]

    one_step(3)
    one_step(0)
    two_step(3)
    one_step(1)
    two_step(0)
    one_step(2)
    two_step(1)
    two_step(2)

    nj = nz // ny
    mine = lax.div(z, ny)

    def z_copy(j):
        return remote(
            z_out.at[j], z_in.at[z], z_s, z_r, (j * ny + b) * 2 + core, rep
        )

    @pl.loop(0, nj - 1)
    def _(i):
        z_copy(lax.rem(mine + farthest(i, nj), nj)).start()

    @pl.when(jnp.logical_not(holder))
    def _():
        z_copy(mine).start()

    def fin_copy(r):
        return remote(fin_out, fin_in.at[a], f_s.at[r], f_r, me, r)

    @pl.when(holder)
    def _():
        z_in[z] = z_out[mine]
        wait_all(z_in, nz - 1, z_r)
        fin_out[...] = jnp.sum(z_in[...].astype(F32), axis=0).astype(BF16)

        @pl.loop(1, n_rep)
        def _(k):
            fin_copy(lax.rem(rep + k, n_rep)).start()

        fin_in[a] = fin_out[...]

    wait_all(got, n_dp - 1, pk_r)
    spread[...] = got[...].astype(F32).reshape(spread.shape)
    for i in range(D // LANES):
        packed[:, i * LANES : (i + 1) * LANES] = spread[
            pl.ds(i, packed.shape[0], stride=D // LANES), :
        ]

    @pl.when(holder)
    def _():
        wait_all(fin_in, nx - 1, f_r)

    @pl.when(jnp.logical_not(holder))
    def _():
        wait_all(fin_in, nx, f_r)

    for s in range(4):
        for i in range(nx):
            piece = fin_in[i, s].astype(F32)
            if s < 3:
                at = s * D + i * LANES
                grad_in[:, at : at + LANES] = piece
            else:
                grad_out[:, i * LANES : (i + 1) * LANES] = piece

    for s in range(4):
        core_copy(s).wait_send()
        for _, copy in one_copies(s):
            copy(line(s, True)[0]).wait_send()
        for _, copy in two_copies(s):
            copy(line(s, False)[0]).wait_send()
    wait_all(send, n_dp - 1, pk_s)

    @pl.when(holder)
    def _():
        wait_all(z_out, nj - 1, z_s)

        @pl.loop(1, n_rep)
        def _(k):
            fin_copy(lax.rem(rep + k, n_rep)).wait_send()

    @pl.when(jnp.logical_not(holder))
    def _():
        wait_all(z_out, nj, z_s)


def place_kernel(*refs):
    count = (len(refs) - 3) // 3
    sources, targets, held = refs[:count], refs[count : 2 * count], refs[2 * count : -3]
    zero, inward, outward = refs[-3:]
    top = sources[0].shape[0]
    here = [
        pltpu.make_async_copy(sources[i], held[i], inward.at[i]) for i in range(count)
    ]
    there = [
        pltpu.make_async_copy(
            held[i], targets[i].at[pl.ds(0, top)] if i == 0 else targets[i], outward.at[i]
        )
        for i in range(count)
    ]
    for copy in here:
        copy.start()
    zero[...] = jnp.zeros_like(zero)
    rest = pltpu.make_async_copy(
        zero, targets[0].at[pl.ds(top, zero.shape[0])], outward.at[count]
    )
    rest.start()
    for i in range(count):
        here[i].wait()
        there[i].start()
    for copy in there:
        copy.wait()
    rest.wait()


def place(home_rows, *results):
    top = results[0].shape[0]
    hbm = pl.BlockSpec(memory_space=pltpu.HBM)
    return pl.pallas_call(
        place_kernel,
        out_shape=(jax.ShapeDtypeStruct((home_rows, D), F32),)
        + tuple(jax.ShapeDtypeStruct(v.shape, v.dtype) for v in results[1:]),
        in_specs=[hbm] * 4,
        out_specs=(hbm,) * 4,
        scratch_shapes=[pltpu.VMEM(v.shape, v.dtype) for v in results]
        + [
            pltpu.VMEM((home_rows - top, D), F32),
            pltpu.SemaphoreType.DMA((4,)),
            pltpu.SemaphoreType.DMA((5,)),
        ],
        name="place",
    )(*results)


def on_device(n_dp, nx, ny, *args):
    nz = n_dp // 2
    deep = nz // ny * SUB
    rows = args[0].shape[0]
    users = args[4].shape
    dma = pltpu.SemaphoreType.DMA
    any_spec = pl.BlockSpec(memory_space=pltpu.HBM)
    vmem = pl.BlockSpec(memory_space=pltpu.VMEM)
    results = pl.pallas_call(
        functools.partial(fused_kernel, n_dp, nx, ny),
        out_shape=(
            jax.ShapeDtypeStruct((TILE, D), F32),
            jax.ShapeDtypeStruct((n_dp * CAP, D), F32),
            jax.ShapeDtypeStruct((SUB, F1), F32),
            jax.ShapeDtypeStruct((SUB, D), F32),
        ),
        in_specs=[any_spec] * 7,
        out_specs=(vmem,) * 4,
        scratch_shapes=[
            pltpu.VMEM((rows, D), BF16),
            pltpu.VMEM((rows, D), BF16),
            pltpu.VMEM((D, F1), F32),
            pltpu.VMEM((D, D), F32),
            pltpu.VMEM(users, jnp.int32),
            pltpu.VMEM(users, jnp.int32),
            pltpu.VMEM(users, jnp.int32),
            pltpu.VMEM((D, F1), BF16),
            pltpu.VMEM((D, D), BF16),
            pltpu.VMEM((rows, F1), F32),
            pltpu.VMEM((rows, D), F32),
            pltpu.VMEM((rows, D), BF16),
            pltpu.VMEM((rows, 256), BF16),
            pltpu.VMEM((rows, 256), BF16),
            pltpu.VMEM((2 * HEADS, TILE, TILE), BF16),
            pltpu.VMEM((2 * HEADS, TILE, TILE), F32),
            pltpu.VMEM((rows, D), F32),
            pltpu.VMEM((rows, F1), BF16),
            pltpu.VMEM((TILE * D // LANES, LANES), F32),
            pltpu.VMEM((n_dp, SUB, LANES), BF16),
            pltpu.VMEM((n_dp, SUB, LANES), BF16),
            pltpu.VMEM((2, 4, ny, nx, deep, LANES), BF16),
            pltpu.VMEM((4, ny, nx, deep, LANES), BF16),
            pltpu.VMEM((4, ny, nx, deep, LANES), BF16),
            pltpu.VMEM((4, nx, ny, deep, LANES), BF16),
            pltpu.VMEM((4, nx, deep, LANES), BF16),
            pltpu.VMEM((4, nx, deep, LANES), BF16),
            pltpu.VMEM((nz // ny, 4, SUB, LANES), BF16),
            pltpu.VMEM((nz, 4, SUB, LANES), BF16),
            pltpu.VMEM((4, SUB, LANES), BF16),
            pltpu.VMEM((nx, 4, SUB, LANES), BF16),
            dma((9,)),
            dma, dma,
            dma((4,)), dma((4,)),
            dma((4, nx)), dma((4, nx)),
            dma((4, nx)), dma((4, nx)),
            dma, dma,
            dma((nx * ny,)), dma,
            pltpu.SemaphoreType.REGULAR,
        ],
        compiler_params=pltpu.CompilerParams(
            collective_id=0, has_side_effects=True, vmem_limit_bytes=58 * 2**20
        ),
        name="fused",
    )(*args)
    return place(rows, *results)


def solution(mesh):
    in_specs = (
        P(("dp", "replica"), None),
        P(("dp", "replica"), None),
        P(),
        P(),
        P(None, "replica", None),
        P(None, "replica", None),
        P(None, "replica", None),
    )
    out_specs = (
        P(("dp", "replica"), None),
        P(("dp", "replica"), None),
        P("dp", None),
        P("dp", None),
    )
    return jax.shard_map(
        functools.partial(on_device, mesh.shape["dp"], 4, mesh.shape["replica"] // 4),
        mesh=mesh,
        in_specs=in_specs,
        out_specs=out_specs,
        check_vma=False,
    )
```

```python
import functools

import jax
import jax.numpy as jnp
from jax import lax
from jax.experimental import pallas as pl
from jax.experimental.pallas import tpu as pltpu
from jax.sharding import PartitionSpec as P

D = 512
HEADS = 4
TILE = 128
CAP = 2
F1 = 1536
LANES = 128
SUB = 8
MESH = pl.DeviceIdType.MESH
F32 = jnp.float32
BF16 = jnp.bfloat16

NT = (((1,), (1,)), ((), ()))
TN = (((0,), (0,)), ((), ()))


def dot(a, b, dims=(((1,), (0,)), ((), ()))):
    return lax.dot_general(a, b, dims, preferred_element_type=F32)


def sigmoid(v):
    return 0.5 * jnp.tanh(0.5 * v) + 0.5


def mean_rows(v):
    return jnp.mean(v, axis=-1, keepdims=True)


def row_norm(v):
    centered = v - mean_rows(v)
    scale = lax.rsqrt(mean_rows(centered * centered) + 1e-05)
    return centered * scale, scale


def norm_back(grad, unit, scale):
    return scale * (grad - mean_rows(grad) - unit * mean_rows(grad * unit))


def fused_kernel(
    n_dp, nx, ny, ev_h, og_h, wi_h, wo_h, ln_h, of_h, tg_h, home, packed, grad_in, grad_out,
    ev, og, wi, wo, ln, of, tg, wib, wob, slope, gate, val, qry, key, wts, wslope, mixed,
    dproj, spread, send, got, parts, core_in, chip, one_in, mid, two_in, z_out, z_in,
    fin_out, fin_in, ld, pk_s, pk_r, c_s, c_r, o_s, o_r, t_s, t_r, z_s, z_r, f_s, f_r, far_sem,
):
    me = lax.axis_index("dp")
    rep = lax.axis_index("replica")
    nz = n_dp // 2
    n_rep = nx * ny
    core = lax.rem(me, 2)
    z = lax.div(me, 2)
    a = lax.rem(rep, nx)
    b = lax.div(rep, nx)
    other = me + 1 - 2 * core
    holder = lax.rem(z, ny) == b

    def load(i, source, target):
        return pltpu.make_async_copy(source, target, ld.at[i])

    def load_w(n):
        cut = pl.ds(n * D, D)
        return load(2 + n, wi_h.at[:, cut], wi.at[:, cut])

    loads = {
        "ev": load(0, ev_h, ev), "wi0": load_w(0), "wi1": load_w(1), "wi2": load_w(2),
        "ln": load(5, ln_h, ln), "of": load(6, of_h, of), "tg": load(7, tg_h, tg),
        "og": load(1, og_h, og), "wo": load(8, wo_h, wo),
    }
    for copy in loads.values():
        copy.start()

    barrier = pltpu.get_barrier_semaphore()

    def farthest(i, count):
        step = lax.div(i + 1, 2)
        return count // 2 + step * (2 * lax.rem(i + 1, 2) - 1)

    jump = n_dp // 4

    @pl.loop(0, jump + 1)
    def _(i):
        for away in (jump + 1 - i, n_dp - jump - 1 + i):
            pl.semaphore_signal(
                barrier, inc=1, device_id=(lax.rem(me + away, n_dp), rep),
                device_id_type=MESH,
            )

    @pl.loop(1, n_rep)
    def _(k):
        pl.semaphore_signal(
            barrier, inc=1, device_id=(me, lax.rem(rep + k, n_rep)), device_id_type=MESH
        )

    def remote(source, target, send_sem, recv_sem, dp, replica):
        return pltpu.make_async_remote_copy(
            src_ref=source, dst_ref=target, send_sem=send_sem, recv_sem=recv_sem,
            device_id=(dp, replica), device_id_type=MESH,
        )

    def wait_all(ref, count, sem):
        part = ref.at[pl.ds(0, count)]
        pltpu.make_async_copy(part, part, sem).wait()

    def core_copy(s):
        return remote(parts.at[1 - core, s], core_in.at[s], c_s.at[s], c_r.at[s], other, rep)

    def line(s, first):
        along_x = (s % 2 == 0) == first
        return (a, nx, lambda q: b * nx + q) if along_x else (b, ny, lambda q: q * nx + a)

    def one_copies(s):
        own, count, rank = line(s, True)
        for k in range(1, count):
            peer = lax.rem(own + k, count)
            block = chip.at[s, :, peer] if s % 2 == 0 else chip.at[s, peer]
            yield peer, lambda slot, block=block, peer=peer: remote(
                block, one_in.at[s, slot], o_s.at[s, peer], o_r.at[s, slot], me, rank(peer)
            )

    def two_copies(s):
        own, count, rank = line(s, False)
        for k in range(1, count):
            peer = lax.rem(own + k, count)
            yield peer, lambda slot, peer=peer: remote(
                mid.at[s, peer], two_in.at[s, slot], t_s.at[s, peer], t_r.at[s, slot],
                me, rank(peer),
            )

    def core_step(s):
        core_copy(s).wait_recv()
        for i in range(ny):
            chip[s, i] = (
                parts[core, s, i].astype(F32) + core_in[s, i].astype(F32)
            ).astype(BF16)
        own = line(s, True)[0]
        for _, copy in one_copies(s):
            copy(own).start()

    def one_step(s):
        own = line(s, True)[0]
        peers = list(one_copies(s))
        for peer, copy in peers:
            copy(peer).wait_recv()
        block = chip[s, :, own] if s % 2 == 0 else chip[s, own]
        total = block.astype(F32)
        for peer, _ in peers:
            total = total + one_in[s, peer].astype(F32)
        mid[s] = total.astype(BF16)
        own = line(s, False)[0]
        for _, copy in two_copies(s):
            copy(own).start()

    def two_step(s):
        own = line(s, False)[0]
        peers = list(two_copies(s))
        for peer, copy in peers:
            copy(peer).wait_recv()
        total = mid[s, own].astype(F32)
        for peer, _ in peers:
            total = total + two_in[s, peer].astype(F32)
        z_out[:, s] = total.reshape(nz // ny, SUB, LANES).astype(BF16)

    rows = lax.broadcasted_iota(jnp.int32, (TILE, 1), 0)
    cols = lax.broadcasted_iota(jnp.int32, (TILE, TILE), 1)
    row2 = lax.broadcasted_iota(jnp.int32, (TILE, TILE), 0)
    low = lax.broadcasted_iota(jnp.int32, (TILE, LANES), 1) < 64
    zero_b = jnp.zeros((TILE, LANES), BF16)
    pair = lax.div(rows, CAP)

    loads["ev"].wait()
    unit, scale = row_norm(ev[...].astype(F32))
    normed = unit.astype(BF16)

    for n in range(0, F1, 256):
        if n % D == 0:
            loads["wi%d" % (n // D)].wait()
        wib[:, n : n + 256] = wi[:, n : n + 256].astype(BF16)
        proj = dot(normed, wib[:, n : n + 256])
        sig = sigmoid(proj)
        act = proj * sig
        slope[:, n : n + 256] = sig + act * (1.0 - sig)
        if n < D:
            gate[:, n : n + 256] = act
        elif n < 2 * D:
            val[:, n - D : n - D + 256] = act.astype(BF16)
        elif n < 2 * D + 256:
            qry[...] = act.astype(BF16)
        else:
            key[...] = act.astype(BF16)

    for name in ("ln", "of", "tg"):
        loads[name].wait()
    ln_row, of_row, tg_row = ln[me], of[me], tg[me]
    users = ln_row.shape[1]
    lanes = lax.broadcasted_iota(jnp.int32, (1, users), 1)
    at_slot = (of_row - TILE) == pair * CAP
    pool_len = jnp.sum(jnp.where(at_slot, ln_row, 0), axis=1, keepdims=True)
    long_len = jnp.broadcast_to(ln_row[:, 0:1], (TILE, 1))
    live_long = rows < long_len
    live_pool = lax.rem(rows, CAP) < pool_len
    live = jnp.concatenate([live_long, live_pool], axis=0)

    for blk in range(2):
        top = blk * TILE
        keep = cols <= row2
        if blk == 0:
            keep = keep & live_long
            size = long_len
        else:
            keep = keep & (lax.div(cols, CAP) == lax.div(row2, CAP)) & live_pool
            size = pool_len
        inv = 1.0 / jnp.maximum(size, 1).astype(F32)
        for h in range(HEADS):
            lane = (h // 2) * LANES
            mine = low if h % 2 == 0 else ~low
            qh = jnp.where(mine, qry[top : top + TILE, lane : lane + LANES], zero_b)
            score = dot(qh, key[top : top + TILE, lane : lane + LANES], NT) * 0.125
            sig = sigmoid(score)
            act = score * sig
            w = jnp.where(keep, act * inv, 0.0).astype(BF16)
            wts[blk * HEADS + h] = w
            wslope[blk * HEADS + h] = jnp.where(
                keep, (sig + act * (1.0 - sig)) * (inv * 0.125), 0.0
            )
            mixed[top : top + TILE, h * LANES : (h + 1) * LANES] = dot(
                w, val[top : top + TILE, h * LANES : (h + 1) * LANES]
            )

    unit_m, scale_m = row_norm(mixed[...])
    hidden = (gate[...] * unit_m).astype(BF16)
    loads["og"].wait()
    grad_live = jnp.where(live, og[...].astype(F32), 0.0)
    grad_b = grad_live.astype(BF16)

    def emit(s, result, first):
        for i in range(result.shape[1] // LANES):
            piece = result[:, i * LANES : (i + 1) * LANES].reshape(
                nz // ny, ny, 2, SUB, LANES
            )
            for c in range(2):
                for g in range(ny):
                    parts[c, s, g, first + i] = (
                        piece[:, g, c].reshape(nz // ny * SUB, LANES).astype(BF16)
                    )

    hidden_t = hidden.T
    for i in range(2):
        emit(3, dot(hidden_t, grad_b[:, i * 256 : i * 256 + 256]), 2 * i)
    pl.semaphore_wait(barrier, 2 * (jump + 1) + n_rep - 1)
    for away in (jump, n_dp - jump):
        pl.semaphore_signal(
            far_sem, inc=1, device_id=(lax.rem(me + away, n_dp), rep), device_id_type=MESH
        )

    core_copy(3).start()

    loads["wo"].wait()
    wob[...] = wo[...].astype(BF16)
    dhid = dot(grad_b, wob[...], NT).astype(BF16).astype(F32)
    dproj[:, :D] = (dhid * unit_m * slope[:, :D]).astype(BF16)
    dmix = norm_back(dhid * gate[...], unit_m, scale_m).astype(BF16)

    normed_t = normed.T

    def in_part(s):
        for i in range(2):
            n = s * D + i * 256
            emit(s, dot(normed_t, dproj[:, n : n + 256]), 2 * i)
        core_copy(s).start()

    in_part(0)

    for blk in range(2):
        top = blk * TILE
        for p in range(HEADS // 2):
            lane = p * LANES
            kk = key[top : top + TILE, lane : lane + LANES]
            qq = qry[top : top + TILE, lane : lane + LANES]
            dq, dk = [], []
            for h in (2 * p, 2 * p + 1):
                dm = dmix[top : top + TILE, h * LANES : (h + 1) * LANES]
                vh = val[top : top + TILE, h * LANES : (h + 1) * LANES]
                w = wts[blk * HEADS + h]
                dw = dot(dm, vh, NT).astype(BF16).astype(F32)
                dv = dot(w, dm, TN).astype(BF16).astype(F32)
                at = D + h * LANES
                dproj[top : top + TILE, at : at + LANES] = (
                    dv * slope[top : top + TILE, at : at + LANES]
                ).astype(BF16)
                ds = (dw * wslope[blk * HEADS + h]).astype(BF16)
                dq.append(dot(ds, kk))
                dk.append(dot(ds, qq, TN))
            for at, pieces in ((2 * D + lane, dq), (2 * D + 256 + lane, dk)):
                both = jnp.where(low, pieces[0], pieces[1]).astype(BF16).astype(F32)
                dproj[top : top + TILE, at : at + LANES] = (
                    both * slope[top : top + TILE, at : at + LANES]
                ).astype(BF16)

    core_step(3)
    core_step(0)
    in_part(1)
    in_part(2)

    dnormed = dot(dproj[...], wib[...], NT).astype(BF16).astype(F32)
    grad = norm_back(dnormed, unit, scale) + grad_live
    grad = jnp.where(live, grad, 0.0)

    to_target = ((tg_row == pair) & (lanes >= 1)).astype(F32).astype(BF16)
    from_slot = at_slot.astype(F32).astype(BF16)
    moves = dot(to_target, from_slot, NT)
    moves = jnp.where(lax.rem(cols, CAP) == lax.rem(row2, CAP), moves, 0.0)
    moved = dot(moves.astype(BF16), grad[TILE:].astype(BF16))
    for i in range(D // LANES):
        spread[pl.ds(i, TILE, stride=D // LANES), :] = moved[:, i * LANES : (i + 1) * LANES]
    send[...] = spread[...].reshape(send.shape).astype(BF16)

    def packed_copy(t):
        return remote(send.at[t], got.at[me], pk_s, pk_r, t, rep)

    core_step(1)
    core_step(2)

    pl.semaphore_wait(far_sem, 2)

    @pl.loop(0, n_dp - 1)
    def _(i):
        packed_copy(lax.rem(me + farthest(i, n_dp), n_dp)).start()

    got[me] = send[me]
    home[...] = grad[:TILE]

    for step in (one_step, two_step):
        for s in (3, 0, 1, 2):
            step(s)

    nj = nz // ny
    mine = lax.div(z, ny)

    def z_copy(j):
        return remote(
            z_out.at[j], z_in.at[z], z_s, z_r, (j * ny + b) * 2 + core, rep
        )

    @pl.loop(0, nj - 1)
    def _(i):
        z_copy(lax.rem(mine + farthest(i, nj), nj)).start()

    @pl.when(jnp.logical_not(holder))
    def _():
        z_copy(mine).start()

    def fin_copy(r):
        return remote(fin_out, fin_in.at[a], f_s.at[r], f_r, me, r)

    @pl.when(holder)
    def _():
        z_in[z] = z_out[mine]
        wait_all(z_in, nz - 1, z_r)
        fin_out[...] = jnp.sum(z_in[...].astype(F32), axis=0).astype(BF16)

        @pl.loop(1, n_rep)
        def _(k):
            fin_copy(lax.rem(rep + k, n_rep)).start()

        fin_in[a] = fin_out[...]

    wait_all(got, n_dp - 1, pk_r)
    spread[...] = got[...].astype(F32).reshape(spread.shape)
    for i in range(D // LANES):
        packed[:, i * LANES : (i + 1) * LANES] = spread[
            pl.ds(i, packed.shape[0], stride=D // LANES), :
        ]

    @pl.when(holder)
    def _():
        wait_all(fin_in, nx - 1, f_r)

    @pl.when(jnp.logical_not(holder))
    def _():
        wait_all(fin_in, nx, f_r)

    for s in range(4):
        for i in range(nx):
            piece = fin_in[i, s].astype(F32)
            if s < 3:
                at = s * D + i * LANES
                grad_in[:, at : at + LANES] = piece
            else:
                grad_out[:, i * LANES : (i + 1) * LANES] = piece

    for s in range(4):
        core_copy(s).wait_send()
        for _, copy in one_copies(s):
            copy(line(s, True)[0]).wait_send()
        for _, copy in two_copies(s):
            copy(line(s, False)[0]).wait_send()
    wait_all(send, n_dp - 1, pk_s)

    @pl.when(holder)
    def _():
        wait_all(z_out, nj - 1, z_s)

        @pl.loop(1, n_rep)
        def _(k):
            fin_copy(lax.rem(rep + k, n_rep)).wait_send()

    @pl.when(jnp.logical_not(holder))
    def _():
        wait_all(z_out, nj, z_s)


def place_kernel(*refs):
    count = (len(refs) - 3) // 3
    sources, targets, held = refs[:count], refs[count : 2 * count], refs[2 * count : -3]
    zero, inward, outward = refs[-3:]
    top = sources[0].shape[0]
    here = [
        pltpu.make_async_copy(sources[i], held[i], inward.at[i]) for i in range(count)
    ]
    there = [
        pltpu.make_async_copy(
            held[i], targets[i].at[pl.ds(0, top)] if i == 0 else targets[i], outward.at[i]
        )
        for i in range(count)
    ]
    for copy in here:
        copy.start()
    zero[...] = jnp.zeros_like(zero)
    rest = pltpu.make_async_copy(
        zero, targets[0].at[pl.ds(top, zero.shape[0])], outward.at[count]
    )
    rest.start()
    for i in range(count):
        here[i].wait()
        there[i].start()
    for copy in there:
        copy.wait()
    rest.wait()


def place(home_rows, *results):
    top = results[0].shape[0]
    hbm = pl.BlockSpec(memory_space=pltpu.HBM)
    return pl.pallas_call(
        place_kernel,
        out_shape=(jax.ShapeDtypeStruct((home_rows, D), F32),)
        + tuple(jax.ShapeDtypeStruct(v.shape, v.dtype) for v in results[1:]),
        in_specs=[hbm] * 4,
        out_specs=(hbm,) * 4,
        scratch_shapes=[pltpu.VMEM(v.shape, v.dtype) for v in results]
        + [
            pltpu.VMEM((home_rows - top, D), F32),
            pltpu.SemaphoreType.DMA((4,)),
            pltpu.SemaphoreType.DMA((5,)),
        ],
        name="place",
    )(*results)


def on_device(n_dp, nx, ny, *args):
    nz = n_dp // 2
    deep = nz // ny * SUB
    rows = args[0].shape[0]
    users = args[4].shape
    dma = pltpu.SemaphoreType.DMA
    any_spec = pl.BlockSpec(memory_space=pltpu.HBM)
    vmem = pl.BlockSpec(memory_space=pltpu.VMEM)
    results = pl.pallas_call(
        functools.partial(fused_kernel, n_dp, nx, ny),
        out_shape=(
            jax.ShapeDtypeStruct((TILE, D), F32),
            jax.ShapeDtypeStruct((n_dp * CAP, D), F32),
            jax.ShapeDtypeStruct((SUB, F1), F32),
            jax.ShapeDtypeStruct((SUB, D), F32),
        ),
        in_specs=[any_spec] * 7,
        out_specs=(vmem,) * 4,
        scratch_shapes=[
            pltpu.VMEM((rows, D), BF16),
            pltpu.VMEM((rows, D), BF16),
            pltpu.VMEM((D, F1), F32),
            pltpu.VMEM((D, D), F32),
            pltpu.VMEM(users, jnp.int32),
            pltpu.VMEM(users, jnp.int32),
            pltpu.VMEM(users, jnp.int32),
            pltpu.VMEM((D, F1), BF16),
            pltpu.VMEM((D, D), BF16),
            pltpu.VMEM((rows, F1), F32),
            pltpu.VMEM((rows, D), F32),
            pltpu.VMEM((rows, D), BF16),
            pltpu.VMEM((rows, 256), BF16),
            pltpu.VMEM((rows, 256), BF16),
            pltpu.VMEM((2 * HEADS, TILE, TILE), BF16),
            pltpu.VMEM((2 * HEADS, TILE, TILE), F32),
            pltpu.VMEM((rows, D), F32),
            pltpu.VMEM((rows, F1), BF16),
            pltpu.VMEM((TILE * D // LANES, LANES), F32),
            pltpu.VMEM((n_dp, SUB, LANES), BF16),
            pltpu.VMEM((n_dp, SUB, LANES), BF16),
            pltpu.VMEM((2, 4, ny, nx, deep, LANES), BF16),
            pltpu.VMEM((4, ny, nx, deep, LANES), BF16),
            pltpu.VMEM((4, ny, nx, deep, LANES), BF16),
            pltpu.VMEM((4, nx, ny, deep, LANES), BF16),
            pltpu.VMEM((4, nx, deep, LANES), BF16),
            pltpu.VMEM((4, nx, deep, LANES), BF16),
            pltpu.VMEM((nz // ny, 4, SUB, LANES), BF16),
            pltpu.VMEM((nz, 4, SUB, LANES), BF16),
            pltpu.VMEM((4, SUB, LANES), BF16),
            pltpu.VMEM((nx, 4, SUB, LANES), BF16),
            dma((9,)),
            dma, dma,
            dma((4,)), dma((4,)),
            dma((4, nx)), dma((4, nx)),
            dma((4, nx)), dma((4, nx)),
            dma, dma,
            dma((nx * ny,)), dma,
            pltpu.SemaphoreType.REGULAR,
        ],
        compiler_params=pltpu.CompilerParams(
            collective_id=0, has_side_effects=True, vmem_limit_bytes=58 * 2**20
        ),
        name="fused",
    )(*args)
    return place(rows, *results)


def solution(mesh):
    in_specs = (
        P(("dp", "replica"), None),
        P(("dp", "replica"), None),
        P(),
        P(),
        P(None, "replica", None),
        P(None, "replica", None),
        P(None, "replica", None),
    )
    out_specs = (
        P(("dp", "replica"), None),
        P(("dp", "replica"), None),
        P("dp", None),
        P("dp", None),
    )
    return jax.shard_map(
        functools.partial(on_device, mesh.shape["dp"], 4, mesh.shape["replica"] // 4),
        mesh=mesh,
        in_specs=in_specs,
        out_specs=out_specs,
        check_vma=False,
    )
```
